128 devices in a mesh: dyn: 8 (over x, core), col: 16 (over z, y).
Axes of the slice: x: 4, y: 4, z: 4, core: 2. Of those that a mesh axis runs over, the one named last changes fastest.
Arguments:
- planck_source: float32 [32, 131072], P(None, ('dyn', 'col')), may hold values from 0.5 to 1.5
- absorber_path: float32 [32, 131072], P(None, ('dyn', 'col')), may hold values from 0.2 to 3
- cloud_depth: float32 [32, 131072], P(None, ('dyn', 'col')), may hold values from 0 to 0.6
- span_map: int32 [131072], P(('dyn', 'col')), may hold values from 0 to 131071, as said below
- surface_source: float32 [131072], P(('dyn', 'col')), may hold values from 0.8 to 1.6
- interp_index: int32 [32, 131072], P(None, ('dyn', 'col')), may hold values from 0 to 830
- interp_weight: bfloat16 [4, 32, 131072], P(None, None, ('dyn', 'col')), may hold values from 0 to 0.5
- sunlit: int32 [131072], P(('dyn', 'col')), may hold values from 0 to 1, as said below
- sw_slot: int32 [131072], P(('dyn', 'col')), may hold values from 0 to 8191, as said below
- cos_zenith: float32 [131072], P(('dyn', 'col')), may hold values from 0.05 to 1
- albedo: float32 [131072], P(('dyn', 'col')), may hold values from 0.05 to 0.8
- table_lw: bfloat16 [256, 896], replicated, may hold values from 0.0029907227 to 3
- table_sw: bfloat16 [224, 896], replicated, may hold values from 0.0029 to 3
- planck_frac: float32 [256], replicated, may hold values from 0.0001 to 0.02
- solar_weight: float32 [224], replicated, may hold values from 0.0001 to 0.02
Outputs:
- heating_lw: float32 [32, 131072], P(None, ('dyn', 'col'))
- heating_sw: float32 [32, 131072], P(None, ('dyn', 'col'))
- sw_surface: float32 [65536], P(('dyn', 'col'))
The draws below stay inside these ranges and needn't reach their ends.
Inputs may be any that keep to these rules, and one draw needn't show every extreme that they name: A permutation of the 131072 physics columns: column i goes to device span_map[i] // 1024 (flat index dyn * 16 + col), position span_map[i] % 1024. The number of columns that device s sends to device t depends only on (t - s) modulo the number of devices, is at most 16, and equals 16 for some pairs. In each dyn row the devices fall into pairs whose sunlit counts add up to 1024, so a dyn row holds 8192 sunlit columns; in every dyn row some device is sunlit in all its columns. For a sunlit column, sw_slot // 512 is the col index of the device of its dyn row that computes its shortwave and sw_slot % 512 its slot there. The sunlit columns of a dyn row, in order of device and column, are dealt to owners in turn from a drawn start; the values are distinct, every owner gets exactly 512, at most 64 from any one device and exactly that many from a fully sunlit one. For dark columns the value is arbitrary.
All inputs are finite; a program needn't handle non-finite values.
Results may differ from the reference program's by a relative error of at most 0.0003.
Values may be sent and summed in bfloat16 or wider, within the bound.
No kernel may reach another device: no remote copies, remote signals or barrier semaphores. Data moves between devices by JAX's collectives and lax.ppermute only.
A program may use at most 128 MiB of HBM per device.

```python
import math
from functools import partial
import jax
import jax.numpy as jnp
from jax import lax

G_LW = 256
G_SW = 224
TEMPS = 14
PRESS = 64
LEV = 32
COL_DEV = 1024
NTAB = 896
COLS = 131072
CAP = 16
SW_DEV = 512
SW_ALL = 65536
N_DYN = 8
N_COL = 16


def shuffled(key, groups, length):
    return jax.vmap(lambda group_key: jax.random.permutation(group_key, length))(jax.random.split(key, groups)).astype(jnp.int32)


def daylight(key):
    subkeys = jax.random.split(key, 6)
    stripes = N_COL
    half_cols = COL_DEV // 2
    shuffle = shuffled(subkeys[0], N_DYN, stripes)
    excess = jax.random.randint(subkeys[1], (N_DYN, stripes // 2), 0, half_cols + 1).astype(jnp.int32)
    excess = excess.at[:, 0].set(half_cols)
    row_ids = jnp.arange(N_DYN, dtype=jnp.int32)[:, None]
    counts = jnp.zeros((N_DYN, stripes), jnp.int32)
    counts = counts.at[row_ids, shuffle[:, :stripes // 2]].set(half_cols + excess)
    counts = counts.at[row_ids, shuffle[:, stripes // 2:]].set(half_cols - excess)
    rank_of = shuffled(subkeys[2], N_DYN * stripes, COL_DEV).reshape(N_DYN, stripes, COL_DEV)
    lighted = (rank_of < counts[:, :, None]).astype(jnp.int32)
    flattened = lighted.reshape(N_DYN, stripes * COL_DEV)
    dealt_rank = jnp.clip(jnp.cumsum(flattened, axis=1) - 1, 0, None)
    offset = jax.random.randint(subkeys[3], (N_DYN, 1), 0, stripes).astype(jnp.int32)
    holder = (dealt_rank + offset) % stripes
    turn_of = jnp.minimum(dealt_rank // stripes, SW_DEV - 1)
    slot_perm = shuffled(subkeys[4], N_DYN * stripes, SW_DEV).reshape(N_DYN, stripes, SW_DEV)
    chosen = slot_perm[row_ids, holder, turn_of]
    filler_slots = jax.random.randint(subkeys[5], (N_DYN, stripes * COL_DEV), 0, stripes * SW_DEV).astype(jnp.int32)
    pairing = jnp.where(flattened == 1, holder * SW_DEV + chosen, filler_slots)
    return (flattened.reshape(-1).astype(jnp.int32), pairing.reshape(-1).astype(jnp.int32))


def draw_sunlit(key, part):
    lighted, pairing = daylight(key)
    return lighted


def draw_sw_slot(key, part):
    lighted, pairing = daylight(key)
    return pairing


def draw_span_map(key, part):
    key = jax.random.fold_in(key, 7)
    subkeys = jax.random.split(key, 4)
    devices = N_DYN * N_COL
    shares = jax.random.randint(subkeys[0], (devices // 2,), 0, CAP + 1).astype(jnp.int32)
    shares = shares.at[0].set(CAP)
    pattern = jnp.stack([shares, CAP - shares], axis=1).reshape(devices)
    pattern = pattern[jax.random.permutation(subkeys[1], devices)]
    senders = jnp.arange(devices, dtype=jnp.int32)
    counts = pattern[(senders[None, :] - senders[:, None]) % devices]
    upper_edge = jnp.cumsum(counts, axis=1)
    column = jnp.arange(COL_DEV, dtype=jnp.int32)
    target = jnp.sum((upper_edge[:, None, :] <= column[None, :, None]).astype(jnp.int32), axis=2)
    within = column[None, :] - jnp.take_along_axis(upper_edge - counts, target, axis=1)
    before = jnp.cumsum(counts, axis=0) - counts
    arrival = jnp.take_along_axis(before, target, axis=1) + within
    landing = shuffled(subkeys[2], devices, COL_DEV)
    placed_at = landing[target, arrival]
    global_slot = target * COL_DEV + placed_at
    mixing = shuffled(subkeys[3], devices, COL_DEV)
    mapped = jnp.take_along_axis(global_slot, mixing, axis=1)
    return mapped.reshape(-1).astype(jnp.int32)


def draw_cloud_depth(key, part):
    key = jax.random.fold_in(key, 11)
    level_key, column_key = jax.random.split(key, 2)
    layer = jax.random.uniform(level_key, (LEV, COLS), jnp.float32, 0.0, 0.6)
    factor = jnp.exp(jax.random.uniform(column_key, (COLS,), jnp.float32, jnp.log(0.01), 0.0))
    return (layer * factor[None, :]).astype(jnp.float32)


def draw_table_sw(key, part):
    key = jax.random.fold_in(key, 13)
    row_key, entry_key = jax.random.split(key, 2)
    floor_value = 0.003
    top = jnp.exp(jax.random.uniform(row_key, (G_SW, 1), jnp.float32, jnp.log(0.005), jnp.log(3.0)))
    spread = jax.random.uniform(entry_key, (G_SW, TEMPS * PRESS), jnp.float32, 0.0, 1.0)
    table = jnp.exp(jnp.log(floor_value) + (jnp.log(top) - jnp.log(floor_value)) * spread)
    return jnp.clip(table, floor_value, 3.0).astype(jnp.bfloat16)


def touch_ends(array, rng, smallest, top_value):
    index_at = [jax.random.randint(jax.random.fold_in(rng, axis), (), 0, length) for axis, length in enumerate(array.shape)]
    longest = array.shape.index(max(array.shape))
    beside = index_at[:longest] + [(index_at[longest] + 1) % array.shape[longest]] + index_at[longest + 1:]
    return array.at[tuple(index_at)].set(smallest).at[tuple(beside)].set(top_value)


def steps_of(own_key, shape, cuts, low, largest):
    gain = 1.0
    for position, shards_of in cuts:
        steps = jax.random.uniform(jax.random.fold_in(jax.random.fold_in(own_key, 6), position), (shards_of,), jnp.float32, low / len(cuts), largest / len(cuts))
        gain = gain * jnp.repeat(jnp.exp(steps), shape[position] // shards_of).reshape((-1,) + (1,) * (len(shape) - 1 - position))
    return gain


def setup_inputs(seed: int = 0) -> dict:
    streams_of = jax.random.split(jax.random.key(seed), 16)
    return {
        "planck_source": jnp.clip(0.5 + 1.0 * jax.random.uniform(streams_of[0], (LEV, COLS), jnp.float32) ** steps_of(streams_of[0], (LEV, COLS), ((1, 128),), -0.2, 0.2), 0.5, 1.5),
        "absorber_path": jnp.clip(jnp.exp(math.log(3.0) - 2.7080502 * jax.random.uniform(streams_of[1], (LEV, COLS), jnp.float32) ** steps_of(streams_of[1], (LEV, COLS), ((1, 128),), -0.2, 0.2)), 0.2, 3.0),
        "cloud_depth": draw_cloud_depth(jax.random.fold_in(streams_of[15], 71), 0),
        "span_map": draw_span_map(jax.random.fold_in(streams_of[15], 71), 0),
        "surface_source": jnp.clip(0.8 + 0.8 * jax.random.uniform(streams_of[4], (COLS,), jnp.float32) ** steps_of(streams_of[4], (COLS,), ((0, 128),), -0.2, 0.2), 0.8, 1.6),
        "interp_index": touch_ends(jax.random.randint(streams_of[5], (LEV, COLS), 0, (TEMPS - 1) * PRESS - 1), jax.random.fold_in(streams_of[5], 1), 0, ((TEMPS - 1) * PRESS - 1) - 1).astype(jnp.int32),
        "interp_weight": jnp.clip(0.5 * jax.random.uniform(streams_of[6], (4, LEV, COLS), jnp.float32) ** steps_of(streams_of[6], (4, LEV, COLS), ((2, 128),), -0.2, 0.2), 0.0, 0.5).astype(jnp.bfloat16),
        "sunlit": draw_sunlit(jax.random.fold_in(streams_of[15], 71), 0),
        "sw_slot": draw_sw_slot(jax.random.fold_in(streams_of[15], 71), 0),
        "cos_zenith": jnp.clip(0.05 + 0.95 * jax.random.uniform(streams_of[9], (COLS,), jnp.float32) ** steps_of(streams_of[9], (COLS,), ((0, 128),), -0.2, 0.2), 0.05, 1.0),
        "albedo": jnp.clip(0.05 + 0.75 * jax.random.uniform(streams_of[10], (COLS,), jnp.float32) ** steps_of(streams_of[10], (COLS,), ((0, 128),), -0.2, 0.2), 0.05, 0.8),
        "table_lw": jnp.clip(jnp.exp(jax.random.uniform(streams_of[11], (G_LW, NTAB), jnp.float32, math.log(0.0029907227), math.log(3.0))), 0.0029907227, 3.0).astype(jnp.bfloat16),
        "table_sw": draw_table_sw(jax.random.fold_in(streams_of[15], 71), 0),
        "planck_frac": jnp.clip(jnp.exp(jax.random.uniform(streams_of[13], (G_LW,), jnp.float32, math.log(0.0001), math.log(0.02))), 0.0001, 0.02),
        "solar_weight": jnp.clip(jnp.exp(jax.random.uniform(streams_of[14], (G_SW,), jnp.float32, math.log(0.0001), math.log(0.02))), 0.0001, 0.02),
    }


def corner_weights(index_row, weight_rows):
    entries = jnp.arange(TEMPS * PRESS, dtype=jnp.int32)[:, None]
    offsets = (0, 1, PRESS, PRESS + 1)
    mixing = jnp.zeros((TEMPS * PRESS, index_row.shape[0]), jnp.bfloat16)
    for corner in range(4):
        matches = entries == (index_row[None, :] + offsets[corner])
        mixing = mixing + jnp.where(matches, weight_rows[corner][None, :], jnp.zeros((), jnp.bfloat16))
    return mixing


def optical_depth(table, index_row, weight_rows, path_row, cloud_row):
    absorb = jnp.dot(table, corner_weights(index_row, weight_rows), preferred_element_type=jnp.float32)
    return path_row[None, :] * absorb + cloud_row[None, :]


def longwave(table, planck_frac, index_cols, weight_cols, path_cols, cloud_cols, planck_cols, surface_cols):
    fraction = planck_frac[:, None]
    weight_levels = jnp.moveaxis(weight_cols, 0, 1)

    def downward(flux_in, inputs):
        index_row, weight_rows, path_row, cloud_row, planck_row = inputs
        optical = optical_depth(table, index_row, weight_rows, path_row, cloud_row)
        transmit = jnp.exp(-1.66 * optical)
        flux_out = flux_in * transmit + fraction * planck_row[None, :] * (1.0 - transmit)
        return flux_out, (transmit, jnp.sum(flux_in - flux_out, axis=0))

    initial = jnp.zeros((table.shape[0], index_cols.shape[1]), jnp.float32)
    bottom_down, (transmits, gained_down) = lax.scan(downward, initial, (index_cols, weight_levels, path_cols, cloud_cols, planck_cols))

    def upward(flux_in, inputs):
        transmit, planck_row = inputs
        flux_out = flux_in * transmit + fraction * planck_row[None, :] * (1.0 - transmit)
        return flux_out, jnp.sum(flux_in - flux_out, axis=0)

    ground = fraction * surface_cols[None, :]
    top_up, gained_up = lax.scan(upward, ground, (transmits, planck_cols), reverse=True)
    return gained_down + gained_up


def shortwave(table, solar_weight, index_cols, weight_cols, path_cols, cloud_cols, cosine_cols, albedo_cols):
    weight_levels = jnp.moveaxis(weight_cols, 0, 1)

    def downward(beam_in, inputs):
        index_row, weight_rows, path_row, cloud_row = inputs
        optical = optical_depth(table, index_row, weight_rows, path_row, cloud_row)
        beam_out = beam_in * jnp.exp(-optical / cosine_cols[None, :])
        return beam_out, (jnp.exp(-1.66 * optical), jnp.sum(beam_in - beam_out, axis=0))

    initial = solar_weight[:, None] * cosine_cols[None, :]
    ground_beam, (diffuse, gained_down) = lax.scan(downward, initial, (index_cols, weight_levels, path_cols, cloud_cols))

    def upward(flux_in, transmit):
        flux_out = flux_in * transmit
        return flux_out, jnp.sum(flux_in - flux_out, axis=0)

    top_up, gained_up = lax.scan(upward, albedo_cols[None, :] * ground_beam, diffuse, reverse=True)
    ground_gain = jnp.sum(ground_beam, axis=0) * (1.0 - albedo_cols)
    return gained_down + gained_up, ground_gain


def by_blocks(function, arrays, block_cols):
    block_count = arrays[0].shape[-1] // block_cols

    def to_blocks(values):
        shaped = values.reshape(values.shape[:-1] + (block_count, block_cols))
        return jnp.moveaxis(shaped, -2, 0)

    def from_blocks(values):
        joined = jnp.moveaxis(values, 0, -2)
        return joined.reshape(joined.shape[:-2] + (block_count * block_cols,))

    results = lax.map(lambda block_args: function(*block_args), tuple(to_blocks(values) for values in arrays))
    return jax.tree.map(from_blocks, results)


def reference(planck_source, absorber_path, cloud_depth, span_map, surface_source, interp_index, interp_weight, sunlit, sw_slot, cos_zenith, albedo, table_lw, table_sw, planck_frac, solar_weight):
    total_cols = span_map.shape[0]
    anchor = jnp.zeros((total_cols,), jnp.int32).at[span_map].set(jnp.arange(total_cols, dtype=jnp.int32))
    planck_phys = jnp.take(planck_source, anchor, axis=1)
    path_phys = jnp.take(absorber_path, anchor, axis=1)
    cloud_phys = jnp.take(cloud_depth, anchor, axis=1)
    lw_heat = by_blocks(partial(longwave, table_lw, planck_frac), (interp_index, interp_weight, path_phys, cloud_phys, planck_phys, surface_source), min(512, COL_DEV))
    row_of = jnp.arange(total_cols, dtype=jnp.int32) // (N_COL * COL_DEV)
    target = jnp.where(sunlit == 1, row_of * (N_COL * SW_DEV) + sw_slot, SW_ALL).astype(jnp.int32)
    chosen = jnp.full((SW_ALL,), total_cols, jnp.int32).at[target].set(jnp.arange(total_cols, dtype=jnp.int32), mode="drop")
    sw_inputs = tuple(jnp.take(values, chosen, axis=-1) for values in (interp_index, interp_weight, path_phys, cloud_phys, cos_zenith, albedo))
    sw_heat, sw_surface = by_blocks(partial(shortwave, table_sw, solar_weight), sw_inputs, min(512, SW_DEV))
    sw_phys = jnp.take(sw_heat, target, axis=1, mode="fill", fill_value=0.0)
    heating_lw = jnp.take(lw_heat, span_map, axis=1)
    heating_sw = jnp.take(sw_phys, span_map, axis=1)
    return heating_lw, heating_sw, sw_surface
```

```python
from functools import partial

import jax
import jax.numpy as jnp
from jax import lax
from jax.experimental import pallas as pl
from jax.experimental.pallas import tpu as pltpu
from jax.sharding import PartitionSpec as P

F32, BF16, I32, I16 = jnp.float32, jnp.bfloat16, jnp.int32, jnp.int16
TEMPS, PRESS, LEV = 14, 64, 32
NTAB = TEMPS * PRESS
KPAD = 1024
CAP = 16
SW_CAP = 64
LOG2E = 1.4426950408889634
DIFF = -1.66 * LOG2E
CODES = ((0.5, 1.0), (0.2, 2.8), (0.0, 0.6))
BLOCK = 256
VMEM_LIMIT = 60 * 1024 * 1024
NT = (((1,), (1,)), ((), ()))
TN = (((0,), (0,)), ((), ()))


def iota(shape, axis, dtype=I32):
    return lax.broadcasted_iota(dtype, shape, axis)


def one_hot(left, right):
    return jnp.where(left == right, 1.0, 0.0).astype(BF16)


def split3(x):
    a = x.astype(BF16)
    rest = x - a.astype(F32)
    b = rest.astype(BF16)
    c = (rest - b.astype(F32)).astype(BF16)
    return a, b, c


def dealt_rank(mark):
    parties, columns = mark.shape
    below = one_hot_less()
    before = jnp.zeros((parties, 1), F32)
    ranks = []
    for k in range(columns // 128):
        part = mark[:, k * 128 : (k + 1) * 128]
        running = jnp.dot(part.astype(BF16), below, preferred_element_type=F32) + before
        ranks.append(jnp.sum(running * part, axis=0, keepdims=True))
        before = before + jnp.sum(part, axis=1, keepdims=True)
    return jnp.concatenate(ranks, axis=1)


def one_hot_less():
    return jnp.where(iota((128, 128), 0) < iota((128, 128), 1), 1.0, 0.0).astype(BF16)


def pack_kernel(planck_ref, path_ref, cloud_ref, map_ref, send_ref, slot_ref):
    columns = map_ref.shape[1]
    devices = send_ref.shape[0] // CAP
    span = map_ref[...]
    shift = columns.bit_length() - 1
    target = lax.shift_right_logical(span, shift)
    mark = jnp.where(iota((devices, columns), 0) == target, 1.0, 0.0)
    slot = target * CAP + dealt_rank(mark).astype(I32)
    slot_ref[...] = slot
    codes = []
    for ref, (low, width) in zip((planck_ref, path_ref, cloud_ref), CODES):
        scaled = (ref[...] - low) * (65535.0 / width) + 0.5
        codes.append(jnp.clip(scaled, 0.0, 65535.0).astype(I32))
    codes.append(jnp.broadcast_to(span & (columns - 1), (LEV, columns)))
    code = jnp.concatenate(codes, axis=0)
    high = lax.shift_right_logical(code, 8).astype(F32).astype(BF16)
    low = (code & 255).astype(F32).astype(BF16)
    both = jnp.concatenate([high, low], axis=0)
    rows = 512
    for k in range(send_ref.shape[0] // rows):
        pick = one_hot(iota((rows, columns), 0) + k * rows, slot)
        got = lax.dot_general(pick, both, NT, preferred_element_type=F32)
        width = 4 * LEV
        value = got[:, :width] * 256.0 + got[:, width:] - 32768.0
        send_ref[pl.ds(k * rows, rows), :] = value.astype(I32).astype(I16)


def radiation_kernel(
    recv_ref,
    surface_ref,
    index_ref,
    weight_ref,
    sunlit_ref,
    slot_ref,
    cosine_ref,
    albedo_ref,
    table_lw_ref,
    table_sw_ref,
    frac_ref,
    solar_ref,
    back_ref,
    ground_ref,
    phys,
    weights,
    planck_ext,
    ratio,
    table,
    mixing,
    absorb,
    transmit,
    state_lw,
    state_sw,
    frac_col,
    solar_col,
    heat,
    gain,
):
    columns = index_ref.shape[1]
    slots = recv_ref.shape[0]
    g_lw, g_sw = table_lw_ref.shape[0], table_sw_ref.shape[0]
    g_all = g_lw + g_sw
    code = recv_ref[...].astype(I32) + 32768
    both = jnp.concatenate(
        [lax.shift_right_logical(code, 8).astype(F32).astype(BF16), (code & 255).astype(F32).astype(BF16)], axis=1
    )
    label = code[:, 3 * LEV : 3 * LEV + 1] - 0
    for k in range(columns // BLOCK):
        pick = one_hot(label, iota((slots, BLOCK), 1) + k * BLOCK)
        got = lax.dot_general(both, pick, TN, preferred_element_type=F32)
        value = got[: 4 * LEV] * 256.0 + got[4 * LEV :]
        for n, (low, width) in enumerate(CODES):
            phys[pl.ds(n * LEV, LEV), pl.ds(k * BLOCK, BLOCK)] = value[n * LEV : (n + 1) * LEV] * (width / 65535.0) + low
    planck = phys[0:LEV, :]
    path = phys[LEV : 2 * LEV, :]
    cloud = phys[2 * LEV : 3 * LEV, :]
    planck_ext[0:1, :] = jnp.zeros((1, columns), F32)
    planck_ext[pl.ds(1, LEV), :] = planck
    planck_ext[pl.ds(LEV + 1, 1), :] = surface_ref[...]
    ratio[...] = cloud / path
    for k in range(4):
        weights[pl.ds(k * LEV, LEV), :] = weight_ref[k].astype(F32)
    ones = jnp.where(iota((g_all, 128), 1) < 3, 1.0, 0.0).astype(BF16)
    table[:g_lw, :NTAB] = table_lw_ref[...]
    table[g_lw:, :NTAB] = table_sw_ref[...]
    table[:, NTAB:] = ones
    mixing[NTAB:, :] = jnp.zeros((KPAD - NTAB, BLOCK), BF16)
    frac = jnp.sum(jnp.where(iota((g_lw, g_lw), 0) == iota((g_lw, g_lw), 1), frac_ref[...], 0.0), axis=1, keepdims=True)
    solar = jnp.sum(jnp.where(iota((g_sw, g_sw), 0) == iota((g_sw, g_sw), 1), solar_ref[...], 0.0), axis=1, keepdims=True)
    frac_col[...] = jnp.broadcast_to(frac, frac_col.shape)
    solar_col[...] = jnp.broadcast_to(solar, solar_col.shape)
    total = jnp.sum(frac_ref[...])
    rows = 32

    def one_block(k, _):
        base = pl.multiple_of(k * BLOCK, BLOCK)
        here = pl.ds(base, BLOCK)
        state_lw[...] = jnp.zeros_like(state_lw)
        cosine = cosine_ref[:, here]
        inverse = -LOG2E / cosine
        top_beam = jnp.zeros((8, BLOCK), F32)
        for r in range(0, g_sw, 8):
            beam = solar_col[r : r + 8, :] * cosine
            state_sw[r : r + 8, :] = beam
            top_beam = top_beam + beam

        def downward(level, before):
            flux_before, beam_before = before
            row = pl.ds(level, 1)
            index = index_ref[row, here]
            temp = lax.shift_right_logical(index, 6).astype(F32).astype(BF16)
            press = index & 63
            w = [weights[pl.ds(c * LEV + level, 1), here] for c in range(4)]
            p_of = iota((PRESS, BLOCK), 0)
            at0, at1 = p_of == press, p_of == press + 1
            low = jnp.where(at0, w[0], jnp.where(at1, w[1], 0.0)).astype(BF16)
            wrap = (p_of == 0) & (press == PRESS - 1)
            high = jnp.where(at0, w[2], jnp.where(at1, w[3], jnp.where(wrap, w[1], 0.0))).astype(BF16)
            over = jnp.where(wrap, w[3], 0.0)[:16].astype(BF16)
            temps = jnp.broadcast_to(temp, (16, BLOCK))
            zero = jnp.zeros((16, BLOCK), BF16)
            is_temp = [temps == jnp.asarray(t, BF16) for t in range(TEMPS)]
            for t in range(TEMPS):
                for p in range(0, PRESS, 16):
                    tile = zero
                    if p == 0 and t >= 2:
                        tile = jnp.where(is_temp[t - 2], over, tile)
                    if t >= 1:
                        tile = jnp.where(is_temp[t - 1], high[p : p + 16], tile)
                    tile = jnp.where(is_temp[t], low[p : p + 16], tile)
                    mixing[t * PRESS + p : t * PRESS + p + 16, :] = tile
            pieces = split3(ratio[row, here])
            tail = [jnp.broadcast_to(x.astype(F32), (16, BLOCK)) for x in pieces]
            which = iota((16, BLOCK), 0)
            mixing[NTAB : NTAB + 16, :] = jnp.where(
                which == 0, tail[0], jnp.where(which == 1, tail[1], jnp.where(which == 2, tail[2], 0.0))
            ).astype(BF16)
            absorb[...] = jnp.dot(table[...], mixing[...], preferred_element_type=F32)
            path_row = phys[pl.ds(LEV + level, 1), here]
            diffuse = path_row * DIFF
            direct = path_row * inverse
            step = planck_ext[pl.ds(level, 1), here] - planck_ext[pl.ds(level + 1, 1), here]
            acc = jnp.zeros((8, BLOCK), F32)
            for r in range(0, g_lw, 8):
                t = jnp.exp2(absorb[r : r + 8, :] * diffuse)
                transmit[level, r : r + 8, :] = t
                e = t * (state_lw[r : r + 8, :] + step)
                state_lw[r : r + 8, :] = e
                acc = acc + e * frac_col[r : r + 8, :]
            acc_sw = jnp.zeros((8, BLOCK), F32)
            for r in range(0, g_sw, 8):
                a = absorb[g_lw + r : g_lw + r + 8, :]
                transmit[level, g_lw + r : g_lw + r + 8, :] = jnp.exp2(a * diffuse)
                b = state_sw[r : r + 8, :] * jnp.exp2(a * direct)
                state_sw[r : r + 8, :] = b
                acc_sw = acc_sw + b
            flux = jnp.sum(acc, axis=0, keepdims=True) + planck_ext[pl.ds(level + 1, 1), here] * total
            beam = jnp.sum(acc_sw, axis=0, keepdims=True)
            heat[row, here] = flux_before - flux
            heat[pl.ds(LEV + level, 1), here] = beam_before - beam
            return flux, beam

        start = (jnp.zeros((1, BLOCK), F32), jnp.sum(top_beam, axis=0, keepdims=True))
        _, ground_beam = lax.fori_loop(0, LEV, downward, start)
        albedo = albedo_ref[:, here]
        gain[0:1, here] = (1.0 - albedo) * ground_beam
        state_lw[...] = jnp.zeros_like(state_lw)
        for r in range(0, g_sw, 8):
            state_sw[r : r + 8, :] = state_sw[r : r + 8, :] * albedo

        def upward(n, before):
            level = LEV - 1 - n
            flux_before, up_before = before
            row = pl.ds(level, 1)
            own = planck_ext[pl.ds(level + 1, 1), here]
            step = planck_ext[pl.ds(level + 2, 1), here] - own
            acc = jnp.zeros((8, BLOCK), F32)
            for r in range(0, g_lw, 8):
                e = transmit[level, r : r + 8, :] * (state_lw[r : r + 8, :] + step)
                state_lw[r : r + 8, :] = e
                acc = acc + e * frac_col[r : r + 8, :]
            acc_sw = jnp.zeros((8, BLOCK), F32)
            for r in range(0, g_sw, 8):
                v = transmit[level, g_lw + r : g_lw + r + 8, :] * state_sw[r : r + 8, :]
                state_sw[r : r + 8, :] = v
                acc_sw = acc_sw + v
            flux = jnp.sum(acc, axis=0, keepdims=True) + own * total
            up = jnp.sum(acc_sw, axis=0, keepdims=True)
            heat[row, here] = heat[row, here] + (flux_before - flux)
            heat[pl.ds(LEV + level, 1), here] = heat[pl.ds(LEV + level, 1), here] + (up_before - up)
            return flux, up

        lax.fori_loop(0, LEV, upward, (surface_ref[:, here] * total, ground_beam * albedo))
        return 0

    lax.fori_loop(0, columns // BLOCK, one_block, 0)

    sunlit = sunlit_ref[...]
    result = jnp.concatenate([heat[0:LEV, :], heat[LEV:, :] * sunlit.astype(F32)], axis=0)
    first = result.astype(BF16)
    second = (result - first.astype(F32)).astype(BF16)
    both = jnp.concatenate([first, second], axis=0)
    rows = 512
    for k in range(slots // rows):
        part = recv_ref[pl.ds(k * rows, rows), :].astype(I32) + 32768
        pick = one_hot(part[:, 3 * LEV : 3 * LEV + 1], iota((rows, columns), 1))
        back_ref[pl.ds(k * rows, rows), :] = lax.dot_general(pick, both, NT, preferred_element_type=F32).astype(BF16)

    owners = ground_ref.shape[0]
    sw_count = columns // 2
    sw_slot = slot_ref[...]
    owner = jnp.where(sunlit == 1, lax.shift_right_logical(sw_slot, sw_count.bit_length() - 1), owners)
    mark = jnp.where(iota((owners, columns), 0) == owner, 1.0, 0.0)
    place = owner * 128 + dealt_rank(mark).astype(I32)
    a, b, c = split3(gain[0:1, :])
    own_slot = sw_slot & (sw_count - 1)
    label_high = lax.shift_right_logical(own_slot, 5).astype(F32) + 1.0
    label_low = (own_slot & 31).astype(F32)
    stack = jnp.zeros((16, columns), F32)
    at = iota((16, columns), 0)
    for n, x in enumerate((a.astype(F32), b.astype(F32), c.astype(F32), label_high, label_low)):
        stack = jnp.where(at == n, x, stack)
    stack = stack.astype(BF16)
    for o in range(owners):
        pick = one_hot(iota((128, columns), 0) + o * 128, place)
        got = lax.dot_general(stack, pick, NT, preferred_element_type=F32)
        value = got[0:1] + got[1:2] + got[2:3]
        label = got[3:4] * 32.0 + got[4:5] - 32.0
        ground_ref[o] = jnp.where(iota((8, 128), 0) == 0, value, label)


def home_kernel(back_ref, slot_ref, lw_ref, sw_ref):
    columns = slot_ref.shape[1]
    slots = back_ref.shape[0]
    got = jnp.zeros((4 * LEV, columns), F32)
    rows = 512
    for k in range(slots // rows):
        pick = one_hot(iota((rows, columns), 0) + k * rows, slot_ref[...])
        got = got + lax.dot_general(back_ref[pl.ds(k * rows, rows), :], pick, TN, preferred_element_type=F32)
    value = got[: 2 * LEV] + got[2 * LEV :]
    lw_ref[...] = value[:LEV]
    sw_ref[...] = value[LEV:]


def surface_kernel(ground_ref, out_ref):
    count = out_ref.shape[1]
    total = jnp.zeros((16, count), F32)
    for o in range(ground_ref.shape[0]):
        got = ground_ref[o]
        pick = one_hot(got[1:2].astype(I32), iota((count, 128), 0))
        a, b, c = split3(got[0:1])
        at = iota((16, 128), 0)
        stack = jnp.where(at == 0, a.astype(F32), jnp.where(at == 1, b.astype(F32), jnp.where(at == 2, c.astype(F32), 0.0)))
        total = total + lax.dot_general(stack.astype(BF16), pick, NT, preferred_element_type=F32)
    out_ref[...] = total[0:1] + total[1:2] + total[2:3]


def params():
    return pltpu.CompilerParams(vmem_limit_bytes=VMEM_LIMIT)


def vmem(count):
    return [pl.BlockSpec(memory_space=pltpu.VMEM)] * count


def body(
    planck_source,
    absorber_path,
    cloud_depth,
    span_map,
    surface_source,
    interp_index,
    interp_weight,
    sunlit,
    sw_slot,
    cos_zenith,
    albedo,
    table_lw,
    table_sw,
    planck_frac,
    solar_weight,
):
    columns = span_map.shape[0]
    owners = lax.axis_size("col")
    devices = lax.axis_size("dyn") * owners
    slots = devices * CAP
    g_lw, g_sw = table_lw.shape[0], table_sw.shape[0]

    def row(x):
        return x.reshape(1, -1)

    send, slot = pl.pallas_call(
        pack_kernel,
        out_shape=(jax.ShapeDtypeStruct((slots, 128), I16), jax.ShapeDtypeStruct((1, columns), I32)),
        in_specs=vmem(4),
        out_specs=tuple(vmem(2)),
        compiler_params=params(),
        name="pack",
    )(planck_source, absorber_path, cloud_depth, row(span_map))
    recv = lax.all_to_all(send.reshape(devices, CAP, 128), ("dyn", "col"), 0, 0, tiled=True)
    back, ground = pl.pallas_call(
        radiation_kernel,
        out_shape=(jax.ShapeDtypeStruct((slots, 128), BF16), jax.ShapeDtypeStruct((owners, 8, 128), F32)),
        in_specs=vmem(12),
        out_specs=tuple(vmem(2)),
        scratch_shapes=[
            pltpu.VMEM((3 * LEV, columns), F32),
            pltpu.VMEM((4 * LEV, columns), F32),
            pltpu.VMEM((40, columns), F32),
            pltpu.VMEM((LEV, columns), F32),
            pltpu.VMEM((g_lw + g_sw, KPAD), BF16),
            pltpu.VMEM((KPAD, BLOCK), BF16),
            pltpu.VMEM((g_lw + g_sw, BLOCK), F32),
            pltpu.VMEM((LEV, g_lw + g_sw, BLOCK), F32),
            pltpu.VMEM((g_lw, BLOCK), F32),
            pltpu.VMEM((g_sw, BLOCK), F32),
            pltpu.VMEM((g_lw, BLOCK), F32),
            pltpu.VMEM((g_sw, BLOCK), F32),
            pltpu.VMEM((2 * LEV, columns), F32),
            pltpu.VMEM((8, columns), F32),
        ],
        compiler_params=params(),
        name="radiation",
    )(
        recv.reshape(slots, 128),
        row(surface_source),
        interp_index,
        interp_weight,
        row(sunlit),
        row(sw_slot),
        row(cos_zenith),
        row(albedo),
        table_lw,
        table_sw,
        row(planck_frac),
        row(solar_weight),
    )
    ground_in = lax.all_to_all(ground, "col", 0, 0, tiled=True)
    home = lax.all_to_all(back.reshape(devices, CAP, 128), ("dyn", "col"), 0, 0, tiled=True)
    surface = pl.pallas_call(
        surface_kernel,
        out_shape=jax.ShapeDtypeStruct((1, columns // 2), F32),
        in_specs=vmem(1),
        out_specs=vmem(1)[0],
        compiler_params=params(),
        name="surface",
    )(ground_in)
    heating_lw, heating_sw = pl.pallas_call(
        home_kernel,
        out_shape=(jax.ShapeDtypeStruct((LEV, columns), F32),) * 2,
        in_specs=vmem(2),
        out_specs=tuple(vmem(2)),
        compiler_params=params(),
        name="home",
    )(home.reshape(slots, 128), slot)
    return (heating_lw, heating_sw, surface.reshape(-1))


def solution(mesh):
    columns = P(None, ("dyn", "col"))
    flat = P(("dyn", "col"))
    in_specs = (
        columns, columns, columns, flat, flat, columns, P(None, None, ("dyn", "col")),
        flat, flat, flat, flat, P(), P(), P(), P(),
    )
    out_specs = (columns, columns, flat)
    return jax.shard_map(body, mesh=mesh, in_specs=in_specs, out_specs=out_specs, check_vma=False)
```

```python
from functools import partial

import jax
import jax.numpy as jnp
from jax import lax
from jax.experimental import pallas as pl
from jax.experimental.pallas import tpu as pltpu
from jax.sharding import PartitionSpec as P

F32, BF16, I32, I16 = jnp.float32, jnp.bfloat16, jnp.int32, jnp.int16
TEMPS, PRESS, LEV = 14, 64, 32
NTAB = TEMPS * PRESS
KPAD = 1024
CAP = 16
SW_CAP = 64
LOG2E = 1.4426950408889634
DIFF = -1.66 * LOG2E
GAIN_SCALE = 8.0
CODES = ((0.5, 1.0), (0.2, 2.8), (0.0, 0.6))
BLOCK = 256
GROUP = 4
VMEM_LIMIT = 60 * 1024 * 1024
NT = (((1,), (1,)), ((), ()))
TN = (((0,), (0,)), ((), ()))


def iota(shape, axis, dtype=I32):
    return lax.broadcasted_iota(dtype, shape, axis)


def one_hot(left, right):
    return jnp.where(left == right, 1.0, 0.0).astype(BF16)


def split3(x):
    a = x.astype(BF16)
    rest = x - a.astype(F32)
    b = rest.astype(BF16)
    c = (rest - b.astype(F32)).astype(BF16)
    return a, b, c


def dealt_rank(mark):
    parties, columns = mark.shape
    below = one_hot_less()
    before = jnp.zeros((parties, 1), F32)
    ranks = []
    for k in range(columns // 128):
        part = mark[:, k * 128 : (k + 1) * 128]
        running = jnp.dot(part.astype(BF16), below, preferred_element_type=F32) + before
        ranks.append(jnp.sum(running * part, axis=0, keepdims=True))
        before = before + jnp.sum(part, axis=1, keepdims=True)
    return jnp.concatenate(ranks, axis=1)


def one_hot_less():
    return jnp.where(iota((128, 128), 0) < iota((128, 128), 1), 1.0, 0.0).astype(BF16)


def pack_kernel(planck_ref, path_ref, cloud_ref, map_ref, send_ref, slot_ref):
    columns = map_ref.shape[1]
    devices = send_ref.shape[0] // CAP
    span = map_ref[...]
    shift = columns.bit_length() - 1
    target = lax.shift_right_logical(span, shift)
    mark = jnp.where(iota((devices, columns), 0) == target, 1.0, 0.0)
    slot = target * CAP + dealt_rank(mark).astype(I32)
    slot_ref[...] = slot
    codes = []
    for ref, (low, width) in zip((planck_ref, path_ref, cloud_ref), CODES):
        scaled = (ref[...] - low) * (65535.0 / width) + 0.5
        codes.append(jnp.clip(scaled, 0.0, 65535.0).astype(I32))
    codes.append(jnp.broadcast_to(span & (columns - 1), (LEV, columns)))
    code = jnp.concatenate(codes, axis=0)
    high = lax.shift_right_logical(code, 8).astype(F32).astype(BF16)
    low = (code & 255).astype(F32).astype(BF16)
    both = jnp.concatenate([high, low], axis=0)
    rows = 512
    for k in range(send_ref.shape[0] // rows):
        pick = one_hot(iota((rows, columns), 0) + k * rows, slot)
        got = lax.dot_general(pick, both, NT, preferred_element_type=F32)
        width = 4 * LEV
        value = got[:, :width] * 256.0 + got[:, width:] - 32768.0
        send_ref[pl.ds(k * rows, rows), :] = value.astype(I32).astype(I16)


def radiation_kernel(
    owners,
    recv_ref,
    surface_ref,
    index_ref,
    weight_ref,
    sunlit_ref,
    slot_ref,
    cosine_ref,
    albedo_ref,
    table_lw_ref,
    table_sw_ref,
    frac_ref,
    solar_ref,
    back_ref,
    phys,
    weights,
    planck_ext,
    ratio,
    table,
    mix_a,
    mix_b,
    out_a,
    out_b,
    transmit,
    down_lw,
    down_sw,
    up_lw,
    up_sw,
    flux,
    frac_col,
    solar_col,
    heat,
    gain,
):
    columns = index_ref.shape[1]
    slots = recv_ref.shape[0]
    g_lw, g_sw = table_lw_ref.shape[0], table_sw_ref.shape[0]
    g_all = g_lw + g_sw
    code = recv_ref[...].astype(I32) + 32768
    both = jnp.concatenate(
        [lax.shift_right_logical(code, 8).astype(F32).astype(BF16), (code & 255).astype(F32).astype(BF16)], axis=1
    )
    label = code[:, 3 * LEV : 3 * LEV + 1] - 0
    for k in range(columns // BLOCK):
        pick = one_hot(label, iota((slots, BLOCK), 1) + k * BLOCK)
        got = lax.dot_general(both, pick, TN, preferred_element_type=F32)
        value = got[: 4 * LEV] * 256.0 + got[4 * LEV :]
        for n, (low, width) in enumerate(CODES):
            phys[pl.ds(n * LEV, LEV), pl.ds(k * BLOCK, BLOCK)] = value[n * LEV : (n + 1) * LEV] * (width / 65535.0) + low
    planck = phys[0:LEV, :]
    path = phys[LEV : 2 * LEV, :]
    cloud = phys[2 * LEV : 3 * LEV, :]
    planck_ext[0:1, :] = jnp.zeros((1, columns), F32)
    planck_ext[pl.ds(1, LEV), :] = planck
    planck_ext[pl.ds(LEV + 1, 1), :] = surface_ref[...]
    ratio[...] = cloud / path
    for k in range(4):
        weights[pl.ds(k * LEV, LEV), :] = weight_ref[k].astype(F32)
    ones = jnp.where(iota((g_all, 128), 1) < 3, 1.0, 0.0).astype(BF16)
    table[:g_lw, :NTAB] = table_lw_ref[...]
    table[g_lw:, :NTAB] = table_sw_ref[...]
    table[:, NTAB:] = ones
    for mix in (mix_a, mix_b):
        mix[NTAB:, :] = jnp.zeros((KPAD - NTAB, GROUP * BLOCK), BF16)
    frac = jnp.sum(jnp.where(iota((g_lw, g_lw), 0) == iota((g_lw, g_lw), 1), frac_ref[...], 0.0), axis=1, keepdims=True)
    solar = jnp.sum(jnp.where(iota((g_sw, g_sw), 0) == iota((g_sw, g_sw), 1), solar_ref[...], 0.0), axis=1, keepdims=True)
    frac_col[...] = jnp.broadcast_to(frac, frac_col.shape)
    solar_col[...] = jnp.broadcast_to(solar, solar_col.shape)
    total = jnp.sum(frac_ref[...])
    levels = GROUP
    per_block = LEV // levels
    width = levels * BLOCK

    def place_of(q):
        base = pl.multiple_of(lax.shift_right_logical(q, per_block.bit_length() - 1) * BLOCK, BLOCK)
        return pl.ds(base, BLOCK), (q & (per_block - 1)) * levels

    def prepare(q, mix, out):
        here, first = place_of(q)
        for n in range(levels):
            level = first + n
            row = pl.ds(level, 1)
            lane = slice(n * BLOCK, (n + 1) * BLOCK)
            index = index_ref[row, here]
            temp = lax.shift_right_logical(index, 6).astype(F32).astype(BF16)
            press = index & 63
            w = [weights[pl.ds(c * LEV + level, 1), here] for c in range(4)]
            p_of = iota((PRESS, BLOCK), 0)
            at0, at1 = p_of == press, p_of == press + 1
            low = jnp.where(at0, w[0], jnp.where(at1, w[1], 0.0)).astype(BF16)
            wrap = (p_of == 0) & (press == PRESS - 1)
            high = jnp.where(at0, w[2], jnp.where(at1, w[3], jnp.where(wrap, w[1], 0.0))).astype(BF16)
            over = jnp.where(wrap, w[3], 0.0)[:16].astype(BF16)
            temps = jnp.broadcast_to(temp, (16, BLOCK))
            zero = jnp.zeros((16, BLOCK), BF16)
            is_temp = [temps == jnp.asarray(t, BF16) for t in range(TEMPS)]
            for t in range(TEMPS):
                for p in range(0, PRESS, 16):
                    tile = zero
                    if p == 0 and t >= 2:
                        tile = jnp.where(is_temp[t - 2], over, tile)
                    if t >= 1:
                        tile = jnp.where(is_temp[t - 1], high[p : p + 16], tile)
                    tile = jnp.where(is_temp[t], low[p : p + 16], tile)
                    mix[t * PRESS + p : t * PRESS + p + 16, lane] = tile
            pieces = split3(ratio[row, here])
            tail = [jnp.broadcast_to(x.astype(F32), (16, BLOCK)) for x in pieces]
            which = iota((16, BLOCK), 0)
            mix[NTAB : NTAB + 16, lane] = jnp.where(
                which == 0, tail[0], jnp.where(which == 1, tail[1], jnp.where(which == 2, tail[2], 0.0))
            ).astype(BF16)
        out[...] = jnp.dot(table[...], mix[...], preferred_element_type=F32)

    def enter_down(q):
        here, _ = place_of(q)
        down_lw[...] = jnp.zeros_like(down_lw)
        cosine = cosine_ref[:, here]
        top_beam = jnp.zeros((8, BLOCK), F32)
        for r in range(0, g_sw, 8):
            beam = solar_col[r : r + 8, :] * cosine
            down_sw[r : r + 8, :] = beam
            top_beam = top_beam + beam
        flux[0:1, :] = jnp.zeros((1, BLOCK), F32)
        flux[1:2, :] = jnp.sum(top_beam, axis=0, keepdims=True)

    def enter_up(q):
        here, _ = place_of(q)
        albedo = albedo_ref[:, here]
        ground_beam = flux[1:2, :]
        gain[0:1, here] = (1.0 - albedo) * ground_beam
        up_lw[...] = jnp.zeros_like(up_lw)
        for r in range(0, g_sw, 8):
            up_sw[r : r + 8, :] = down_sw[r : r + 8, :] * albedo
        flux[2:3, :] = surface_ref[:, here] * total
        flux[3:4, :] = ground_beam * albedo

    def downward(q, out):
        here, first = place_of(q)
        half = lax.shift_right_logical(q, per_block.bit_length() - 1) & 1
        inverse = -LOG2E / cosine_ref[:, here]
        diffuse, direct, step, own = [], [], [], []
        for n in range(levels):
            path_row = phys[pl.ds(LEV + first + n, 1), here]
            diffuse.append(path_row * DIFF)
            direct.append(path_row * inverse)
            own.append(planck_ext[pl.ds(first + n + 1, 1), here])
            step.append(planck_ext[pl.ds(first + n, 1), here] - own[-1])
        acc = [jnp.zeros((8, BLOCK), F32)] * levels
        for r in range(0, g_lw, 8):
            e = down_lw[r : r + 8, :]
            frac_here = frac_col[r : r + 8, :]
            for n in range(levels):
                t = jnp.exp2(out[r : r + 8, n * BLOCK : (n + 1) * BLOCK] * diffuse[n])
                transmit[half, first + n, r : r + 8, :] = t
                e = t * (e + step[n])
                acc[n] = acc[n] + e * frac_here
            down_lw[r : r + 8, :] = e
        acc_sw = [jnp.zeros((8, BLOCK), F32)] * levels
        for r in range(0, g_sw, 8):
            b = down_sw[r : r + 8, :]
            for n in range(levels):
                x = out[g_lw + r : g_lw + r + 8, n * BLOCK : (n + 1) * BLOCK]
                transmit[half, first + n, g_lw + r : g_lw + r + 8, :] = jnp.exp2(x * diffuse[n])
                b = b * jnp.exp2(x * direct[n])
                acc_sw[n] = acc_sw[n] + b
            down_sw[r : r + 8, :] = b
        lw, sw = flux[0:1, :], flux[1:2, :]
        for n in range(levels):
            new_lw = jnp.sum(acc[n], axis=0, keepdims=True) + own[n] * total
            new_sw = jnp.sum(acc_sw[n], axis=0, keepdims=True)
            heat[pl.ds(first + n, 1), here] = lw - new_lw
            heat[pl.ds(LEV + first + n, 1), here] = sw - new_sw
            lw, sw = new_lw, new_sw
        flux[0:1, :] = lw
        flux[1:2, :] = sw

    def upward(q):
        here, first = place_of(q)
        half = lax.shift_right_logical(q, per_block.bit_length() - 1) & 1
        last = LEV - 1 - first
        step, own = [], []
        for n in range(levels):
            own.append(planck_ext[pl.ds(last - n + 1, 1), here])
            step.append(planck_ext[pl.ds(last - n + 2, 1), here] - own[-1])
        acc = [jnp.zeros((8, BLOCK), F32)] * levels
        for r in range(0, g_lw, 8):
            e = up_lw[r : r + 8, :]
            frac_here = frac_col[r : r + 8, :]
            for n in range(levels):
                e = transmit[half, last - n, r : r + 8, :] * (e + step[n])
                acc[n] = acc[n] + e * frac_here
            up_lw[r : r + 8, :] = e
        acc_sw = [jnp.zeros((8, BLOCK), F32)] * levels
        for r in range(0, g_sw, 8):
            v = up_sw[r : r + 8, :]
            for n in range(levels):
                v = transmit[half, last - n, g_lw + r : g_lw + r + 8, :] * v
                acc_sw[n] = acc_sw[n] + v
            up_sw[r : r + 8, :] = v
        lw, sw = flux[2:3, :], flux[3:4, :]
        for n in range(levels):
            new_lw = jnp.sum(acc[n], axis=0, keepdims=True) + own[n] * total
            new_sw = jnp.sum(acc_sw[n], axis=0, keepdims=True)
            row, row_sw = pl.ds(last - n, 1), pl.ds(LEV + last - n, 1)
            heat[row, here] = heat[row, here] + (lw - new_lw)
            heat[row_sw, here] = heat[row_sw, here] + (sw - new_sw)
            lw, sw = new_lw, new_sw
        flux[2:3, :] = lw
        flux[3:4, :] = sw

    groups = per_block * (columns // BLOCK)

    def first_block(i, _):
        q = 2 * i
        prepare(q + 1, mix_b, out_b)
        downward(q, out_a)
        prepare(q + 2, mix_a, out_a)
        downward(q + 1, out_b)
        return 0

    def later_block(i, _):
        q = 2 * i

        @pl.when((q & (per_block - 1)) == 0)
        def _():
            enter_up(q - per_block)
            enter_down(q)

        upward(q - per_block)
        prepare(q + 1, mix_b, out_b)
        downward(q, out_a)
        upward(q + 1 - per_block)
        prepare(jnp.minimum(q + 2, groups - 1), mix_a, out_a)
        downward(q + 1, out_b)
        return 0

    def last_up(i, _):
        upward(i)
        return 0

    enter_down(0)
    prepare(0, mix_a, out_a)
    lax.fori_loop(0, per_block // 2, first_block, 0)
    lax.fori_loop(per_block // 2, groups // 2, later_block, 0)
    enter_up(groups - per_block)
    lax.fori_loop(groups - per_block, groups, last_up, 0)

    devices = slots // CAP
    half_rows = devices * CAP // 2
    sunlit = sunlit_ref[...]
    result = jnp.concatenate([heat[0:LEV, :], heat[LEV:, :] * sunlit.astype(F32)], axis=0)
    largest = jnp.max(jnp.abs(result), axis=1, keepdims=True)
    scale_code = jnp.ceil(jnp.log2(jnp.maximum(largest, 1e-30)) * 256.0 + 0.5)
    codes = result * (32767.0 * jnp.exp2(scale_code * (-1.0 / 256.0))) + 32768.5
    codes = jnp.clip(codes, 0.0, 65535.0).astype(I32)
    high = lax.shift_right_logical(codes, 8).astype(F32)
    low = (codes & 255).astype(F32)
    none = jnp.zeros_like(high)
    left = jnp.concatenate([high, none, low, none], axis=0).astype(BF16)
    right = jnp.concatenate([none, high, none, low], axis=0).astype(BF16)
    lanes = 4 * LEV
    diagonal = iota((2 * LEV, lanes), 0) == (iota((2 * LEV, lanes), 1) & (2 * LEV - 1))
    scale_row = jnp.sum(jnp.where(diagonal, scale_code, 0.0), axis=0, keepdims=True).astype(I32)

    sw_count = columns // 2
    sw_slot = slot_ref[...]
    owner = jnp.where(sunlit == 1, lax.shift_right_logical(sw_slot, sw_count.bit_length() - 1), owners)
    mark = jnp.where(iota((owners, columns), 0) == owner, 1.0, 0.0)
    place = owner * SW_CAP + dealt_rank(mark).astype(I32)
    scaled = gain[0:1, :] * (1.0 / GAIN_SCALE)
    first = jnp.floor(scaled * 32768.0)
    second = jnp.floor((scaled * 32768.0 - first) * 32768.0)
    first, second = first.astype(I32), second.astype(I32)
    own_slot = sw_slot & (sw_count - 1)
    pieces = [first, second, own_slot + 1]
    stack = jnp.zeros((16, columns), F32)
    at = iota((16, columns), 0)
    for n, x in enumerate(pieces):
        stack = jnp.where(at == 2 * n, lax.shift_right_logical(x, 8).astype(F32), stack)
        stack = jnp.where(at == 2 * n + 1, (x & 255).astype(F32), stack)
    stack = stack.astype(BF16)
    extras = []
    for o in range(0, owners, 2):
        pick = one_hot(iota((2 * SW_CAP, columns), 0) + o * SW_CAP, place)
        got = lax.dot_general(stack, pick, NT, preferred_element_type=F32)
        row_of = iota((8, lanes), 0)
        rows = [scale_row] + [
            (got[2 * n : 2 * n + 1] * 256.0 + got[2 * n + 1 : 2 * n + 2]).astype(I32) for n in range(3)
        ]
        both = jnp.zeros((8, lanes), I32)
        for n, x in enumerate(rows):
            both = jnp.where(row_of == n, x, both)
        extras += [both, both]
    extras = jnp.stack(extras)

    step = 256
    for k in range(half_rows // step):
        part = recv_ref[pl.ds(2 * k * step, 2 * step), :].astype(I32) + 32768
        label = jnp.broadcast_to(part[:, 3 * LEV : 3 * LEV + 1], (2 * step, 128)).reshape(2 * step // CAP, CAP, 128)
        got = jnp.zeros((step, 2 * lanes), F32)
        for side, value in enumerate((left, right)):
            mine = label[:, 8 * side : 8 * side + 8, :].reshape(step, 128)
            pick = jnp.concatenate(
                [one_hot(mine, iota((step, 128), 1) + c * 128) for c in range(columns // 128)], axis=1
            )
            got = got + lax.dot_general(pick, value, NT, preferred_element_type=F32)
        code = (got[:, :lanes] * 256.0 + got[:, lanes:]).astype(I32) - 32768
        code = code.reshape(step // 8, 8, lanes)
        more = jnp.concatenate([extras] * (step // 8 // owners), axis=0)
        out = jnp.concatenate([code, more], axis=1).reshape(2 * step, lanes)
        back_ref[pl.ds(2 * k * step, 2 * step), :] = out.astype(I16)


def home_kernel(back_ref, slot_ref, row_ref, lw_ref, sw_ref, surface_ref):
    columns = slot_ref.shape[1]
    slots = back_ref.shape[0]
    slot = slot_ref[...]
    got = jnp.zeros((4 * LEV, columns), F32)
    step = 256
    wide = 2 * LEV
    for k in range(slots // 2 // step):
        part = back_ref[pl.ds(2 * k * step, 2 * step), :].astype(I32).reshape(2 * step // CAP, CAP, 128)
        scale = jnp.exp2(part[:, 8:9, :].astype(F32) * (1.0 / 256.0)) * (1.0 / 32767.0)
        value = (part[:, :8, :].astype(F32) * scale).reshape(step, 128)
        first = value.astype(BF16)
        second = (value - first.astype(F32)).astype(BF16)
        row_of = iota((step, columns), 0) + k * step
        first_slot = lax.shift_right_logical(row_of, 3) * CAP + (row_of & 7)
        for side in range(2):
            pick = one_hot(first_slot + 8 * side, slot)
            lane = slice(side * wide, (side + 1) * wide)
            both = jnp.concatenate([first[:, lane], second[:, lane]], axis=1)
            got = got + lax.dot_general(both, pick, TN, preferred_element_type=F32)
    value = got[:wide] + got[wide:]
    lw_ref[...] = value[:LEV]
    sw_ref[...] = value[LEV:]

    count = surface_ref.shape[1]
    owners = 16
    mine = row_ref[0] * (owners * CAP)
    total = jnp.zeros((16, count), F32)
    odd = (row_ref[1] & 1) == 1
    for o in range(owners):
        got = back_ref[pl.ds(pl.multiple_of(mine + o * CAP, CAP), CAP), :].astype(I32)
        first, second, label = got[9:10], got[10:11], got[11:12]
        value = (first.astype(F32) + second.astype(F32) * (1.0 / 32768.0)) * (GAIN_SCALE / 32768.0)
        lane = iota((1, 128), 1)
        value = jnp.where((lane >= SW_CAP) == odd, value, 0.0)
        pick = one_hot(label - 1, iota((count, 128), 0))
        a, b, c = split3(value)
        at = iota((16, 128), 0)
        stack = jnp.where(
            at == 0, a.astype(F32), jnp.where(at == 1, b.astype(F32), jnp.where(at == 2, c.astype(F32), 0.0))
        )
        total = total + lax.dot_general(stack.astype(BF16), pick, NT, preferred_element_type=F32)
    surface_ref[...] = total[0:1] + total[1:2] + total[2:3]


def params():
    return pltpu.CompilerParams(vmem_limit_bytes=VMEM_LIMIT)


def vmem(count):
    return [pl.BlockSpec(memory_space=pltpu.VMEM)] * count


def body(
    planck_source,
    absorber_path,
    cloud_depth,
    span_map,
    surface_source,
    interp_index,
    interp_weight,
    sunlit,
    sw_slot,
    cos_zenith,
    albedo,
    table_lw,
    table_sw,
    planck_frac,
    solar_weight,
):
    columns = span_map.shape[0]
    owners = lax.axis_size("col")
    devices = lax.axis_size("dyn") * owners
    slots = devices * CAP
    g_lw, g_sw = table_lw.shape[0], table_sw.shape[0]

    def row(x):
        return x.reshape(1, -1)

    send, slot = pl.pallas_call(
        pack_kernel,
        out_shape=(jax.ShapeDtypeStruct((slots, 128), I16), jax.ShapeDtypeStruct((1, columns), I32)),
        in_specs=vmem(4),
        out_specs=tuple(vmem(2)),
        compiler_params=params(),
        name="pack",
    )(planck_source, absorber_path, cloud_depth, row(span_map))
    recv = lax.all_to_all(send.reshape(devices, CAP, 128), ("dyn", "col"), 0, 0, tiled=True)
    back = pl.pallas_call(
        partial(radiation_kernel, owners),
        out_shape=jax.ShapeDtypeStruct((slots, 128), I16),
        in_specs=vmem(12),
        out_specs=vmem(1)[0],
        scratch_shapes=[
            pltpu.VMEM((3 * LEV, columns), F32),
            pltpu.VMEM((4 * LEV, columns), F32),
            pltpu.VMEM((40, columns), F32),
            pltpu.VMEM((LEV, columns), F32),
            pltpu.VMEM((g_lw + g_sw, KPAD), BF16),
            pltpu.VMEM((KPAD, GROUP * BLOCK), BF16),
            pltpu.VMEM((KPAD, GROUP * BLOCK), BF16),
            pltpu.VMEM((g_lw + g_sw, GROUP * BLOCK), F32),
            pltpu.VMEM((g_lw + g_sw, GROUP * BLOCK), F32),
            pltpu.VMEM((2, LEV, g_lw + g_sw, BLOCK), F32),
            pltpu.VMEM((g_lw, BLOCK), F32),
            pltpu.VMEM((g_sw, BLOCK), F32),
            pltpu.VMEM((g_lw, BLOCK), F32),
            pltpu.VMEM((g_sw, BLOCK), F32),
            pltpu.VMEM((8, BLOCK), F32),
            pltpu.VMEM((g_lw, BLOCK), F32),
            pltpu.VMEM((g_sw, BLOCK), F32),
            pltpu.VMEM((2 * LEV, columns), F32),
            pltpu.VMEM((8, columns), F32),
        ],
        compiler_params=params(),
        name="radiation",
    )(
        recv.reshape(slots, 128),
        row(surface_source),
        interp_index,
        interp_weight,
        row(sunlit),
        row(sw_slot),
        row(cos_zenith),
        row(albedo),
        table_lw,
        table_sw,
        row(planck_frac),
        row(solar_weight),
    )
    home = lax.all_to_all(back.reshape(devices, CAP, 128), ("dyn", "col"), 0, 0, tiled=True)
    place = jnp.stack([lax.axis_index("dyn"), lax.axis_index("col")]).astype(I32)
    heating_lw, heating_sw, surface = pl.pallas_call(
        home_kernel,
        out_shape=(jax.ShapeDtypeStruct((LEV, columns), F32),) * 2
        + (jax.ShapeDtypeStruct((1, columns // 2), F32),),
        in_specs=vmem(2) + [pl.BlockSpec(memory_space=pltpu.SMEM)],
        out_specs=tuple(vmem(3)),
        compiler_params=params(),
        name="home",
    )(home.reshape(slots, 128), slot, place)
    return (heating_lw, heating_sw, surface.reshape(-1))


def solution(mesh):
    columns = P(None, ("dyn", "col"))
    flat = P(("dyn", "col"))
    in_specs = (
        columns, columns, columns, flat, flat, columns, P(None, None, ("dyn", "col")),
        flat, flat, flat, flat, P(), P(), P(), P(),
    )
    out_specs = (columns, columns, flat)
    return jax.shard_map(body, mesh=mesh, in_specs=in_specs, out_specs=out_specs, check_vma=False)
```

```python
from functools import partial

import jax
import jax.numpy as jnp
from jax import lax
from jax.experimental import pallas as pl
from jax.experimental.pallas import tpu as pltpu
from jax.sharding import PartitionSpec as P

F32, BF16, I32, I16 = jnp.float32, jnp.bfloat16, jnp.int32, jnp.int16
TEMPS, PRESS, LEV = 14, 64, 32
NTAB = TEMPS * PRESS
KPAD = 1024
CAP = 16
SW_CAP = 64
LOG2E = 1.4426950408889634
DIFF = -1.66 * LOG2E
GAIN_SCALE = 8.0
CODES = ((0.5, 1.0), (0.2, 2.8), (0.0, 0.6))
BLOCK = 256
GROUP = 4
EARLY = 2
VMEM_LIMIT = 60 * 1024 * 1024
NT = (((1,), (1,)), ((), ()))
TN = (((0,), (0,)), ((), ()))


def iota(shape, axis, dtype=I32):
    return lax.broadcasted_iota(dtype, shape, axis)


def one_hot(left, right):
    return jnp.where(left == right, 1.0, 0.0).astype(BF16)


def split3(x):
    a = x.astype(BF16)
    rest = x - a.astype(F32)
    b = rest.astype(BF16)
    c = (rest - b.astype(F32)).astype(BF16)
    return a, b, c


def dealt_rank(mark):
    parties, columns = mark.shape
    below = one_hot_less()
    before = jnp.zeros((parties, 1), F32)
    ranks = []
    for k in range(columns // 128):
        part = mark[:, k * 128 : (k + 1) * 128]
        running = jnp.dot(part.astype(BF16), below, preferred_element_type=F32) + before
        ranks.append(jnp.sum(running * part, axis=0, keepdims=True))
        before = before + jnp.sum(part, axis=1, keepdims=True)
    return jnp.concatenate(ranks, axis=1)


def one_hot_less():
    return jnp.where(iota((128, 128), 0) < iota((128, 128), 1), 1.0, 0.0).astype(BF16)


def mix_level(index, weight_rows, mix, lane):
    wide = index.shape[1]

    def spread(x):
        return jnp.broadcast_to(x.astype(F32).astype(BF16), (16, wide))

    temp = spread(lax.shift_right_logical(index, 6))
    press = spread(index & (PRESS - 1))
    after = press + jnp.asarray(1, BF16)
    w = [spread(x) for x in weight_rows]
    zero = jnp.zeros((16, wide), BF16)
    at = iota((16, wide), 0).astype(F32).astype(BF16)
    low, high = [], []
    for p in range(0, PRESS, 16):
        here = at + jnp.asarray(p, BF16)
        at0, at1 = here == press, here == after
        low.append(jnp.where(at0, w[0], jnp.where(at1, w[1], zero)))
        high.append(jnp.where(at0, w[2], jnp.where(at1, w[3], zero)))
    wrap = at == press - jnp.asarray(PRESS - 1, BF16)
    high[0] = jnp.where(wrap, w[1], high[0])
    over = jnp.where(wrap, w[3], zero)
    for t in range(TEMPS):
        is_temp = [temp == jnp.asarray(t - d, BF16) for d in range(3)]
        for n in range(PRESS // 16):
            tile = zero
            if n == 0 and t >= 2:
                tile = jnp.where(is_temp[2], over, tile)
            if t >= 1:
                tile = jnp.where(is_temp[1], high[n], tile)
            tile = jnp.where(is_temp[0], low[n], tile)
            first = t * PRESS + n * 16
            mix[first : first + 16, lane] = tile


def absorb_kernel(index_ref, weight_ref, table_lw_ref, table_sw_ref, out_ref, weights, table, mix):
    g_lw = table_lw_ref.shape[0]
    step = pl.program_id(0)

    @pl.when(step == 0)
    def _():
        for k in range(4):
            weights[pl.ds(k * LEV, LEV), :] = weight_ref[k].astype(F32)
        table[:g_lw, :] = table_lw_ref[...]
        table[g_lw:, :] = table_sw_ref[...]

    units = out_ref.shape[0]
    for u in range(units):
        unit = step * units + u
        per = LEV // (2 * GROUP)
        here = pl.ds(pl.multiple_of(unit // per * BLOCK, BLOCK), BLOCK)
        for n in range(EARLY):
            level = (unit % per) * 2 * GROUP + 2 * GROUP - EARLY + n
            row = pl.ds(level, 1)
            lane = slice((u * EARLY + n) * BLOCK, (u * EARLY + n + 1) * BLOCK)
            mix_level(index_ref[row, here], [weights[pl.ds(c * LEV + level, 1), here] for c in range(4)], mix, lane)
    got = jnp.dot(table[...], mix[...], preferred_element_type=F32)
    for u in range(units):
        out_ref[u] = got[:, u * EARLY * BLOCK : (u + 1) * EARLY * BLOCK]


def pack_kernel(planck_ref, path_ref, cloud_ref, map_ref, send_ref, slot_ref):
    columns = map_ref.shape[1]
    devices = send_ref.shape[0] // CAP
    span = map_ref[...]
    shift = columns.bit_length() - 1
    target = lax.shift_right_logical(span, shift)
    mark = jnp.where(iota((devices, columns), 0) == target, 1.0, 0.0)
    slot = target * CAP + dealt_rank(mark).astype(I32)
    slot_ref[...] = slot
    codes = []
    for ref, (low, width) in zip((planck_ref, path_ref, cloud_ref), CODES):
        scaled = (ref[...] - low) * (65535.0 / width) + 0.5
        codes.append(jnp.clip(scaled, 0.0, 65535.0).astype(I32))
    codes.append(jnp.broadcast_to(span & (columns - 1), (LEV, columns)))
    code = jnp.concatenate(codes, axis=0)
    high = lax.shift_right_logical(code, 8).astype(F32).astype(BF16)
    low = (code & 255).astype(F32).astype(BF16)
    both = jnp.concatenate([high, low], axis=0)
    rows = 512
    for k in range(send_ref.shape[0] // rows):
        pick = one_hot(iota((rows, columns), 0) + k * rows, slot)
        got = lax.dot_general(pick, both, NT, preferred_element_type=F32)
        width = 4 * LEV
        value = got[:, :width] * 256.0 + got[:, width:] - 32768.0
        send_ref[pl.ds(k * rows, rows), :] = value.astype(I32).astype(I16)


def radiation_kernel(
    owners,
    recv_ref,
    pre_ref,
    surface_ref,
    index_ref,
    weight_ref,
    sunlit_ref,
    slot_ref,
    cosine_ref,
    albedo_ref,
    table_lw_ref,
    table_sw_ref,
    frac_ref,
    solar_ref,
    back_ref,
    phys,
    weights,
    planck_ext,
    ratio,
    table,
    mix_a,
    mix_b,
    out_a,
    out_b,
    transmit,
    down_lw,
    down_sw,
    up_lw,
    up_sw,
    flux,
    frac_col,
    solar_col,
    heat,
    gain,
    pre_buf,
    pre_sem,
):
    columns = index_ref.shape[1]
    slots = recv_ref.shape[0]
    g_lw, g_sw = table_lw_ref.shape[0], table_sw_ref.shape[0]
    g_all = g_lw + g_sw
    first_fetch = pltpu.make_async_copy(pre_ref.at[0], pre_buf.at[0], pre_sem.at[0])
    first_fetch.start()
    code = recv_ref[...].astype(I32) + 32768
    both = jnp.concatenate(
        [lax.shift_right_logical(code, 8).astype(F32).astype(BF16), (code & 255).astype(F32).astype(BF16)], axis=1
    )
    label = code[:, 3 * LEV : 3 * LEV + 1] - 0
    for k in range(columns // BLOCK):
        pick = one_hot(label, iota((slots, BLOCK), 1) + k * BLOCK)
        got = lax.dot_general(both, pick, TN, preferred_element_type=F32)
        value = got[: 4 * LEV] * 256.0 + got[4 * LEV :]
        for n, (low, width) in enumerate(CODES):
            phys[pl.ds(n * LEV, LEV), pl.ds(k * BLOCK, BLOCK)] = value[n * LEV : (n + 1) * LEV] * (width / 65535.0) + low
    planck = phys[0:LEV, :]
    path = phys[LEV : 2 * LEV, :]
    cloud = phys[2 * LEV : 3 * LEV, :]
    planck_ext[0:1, :] = jnp.zeros((1, columns), F32)
    planck_ext[pl.ds(1, LEV), :] = planck
    planck_ext[pl.ds(LEV + 1, 1), :] = surface_ref[...]
    ratio[...] = cloud / path
    for k in range(4):
        weights[pl.ds(k * LEV, LEV), :] = weight_ref[k].astype(F32)
    ones = jnp.where(iota((g_all, 128), 1) < 3, 1.0, 0.0).astype(BF16)
    table[:g_lw, :NTAB] = table_lw_ref[...]
    table[g_lw:, :NTAB] = table_sw_ref[...]
    table[:, NTAB:] = ones
    for mix in (mix_a, mix_b):
        mix[NTAB:, :] = jnp.zeros((KPAD - NTAB, mix.shape[1]), BF16)
    frac = jnp.sum(jnp.where(iota((g_lw, g_lw), 0) == iota((g_lw, g_lw), 1), frac_ref[...], 0.0), axis=1, keepdims=True)
    solar = jnp.sum(jnp.where(iota((g_sw, g_sw), 0) == iota((g_sw, g_sw), 1), solar_ref[...], 0.0), axis=1, keepdims=True)
    frac_col[...] = jnp.broadcast_to(frac, frac_col.shape)
    solar_col[...] = jnp.broadcast_to(solar, solar_col.shape)
    total = jnp.sum(frac_ref[...])
    levels = GROUP
    per_block = LEV // levels
    width = levels * BLOCK

    def place_of(q):
        base = pl.multiple_of(lax.shift_right_logical(q, per_block.bit_length() - 1) * BLOCK, BLOCK)
        return pl.ds(base, BLOCK), (q & (per_block - 1)) * levels

    def prepare(q, mix, out, count=GROUP):
        here, first = place_of(q)
        for n in range(count):
            level = first + n
            row = pl.ds(level, 1)
            lane = slice(n * BLOCK, (n + 1) * BLOCK)
            mix_level(index_ref[row, here], [weights[pl.ds(c * LEV + level, 1), here] for c in range(4)], mix, lane)
            pieces = split3(ratio[row, here])
            tail = [jnp.broadcast_to(x.astype(F32), (16, BLOCK)) for x in pieces]
            which = iota((16, BLOCK), 0)
            mix[NTAB : NTAB + 16, lane] = jnp.where(
                which == 0, tail[0], jnp.where(which == 1, tail[1], jnp.where(which == 2, tail[2], 0.0))
            ).astype(BF16)
        out[...] = jnp.dot(table[...], mix[...], preferred_element_type=F32)

    def enter_down(q):
        here, _ = place_of(q)
        down_lw[...] = jnp.zeros_like(down_lw)
        cosine = cosine_ref[:, here]
        top_beam = jnp.zeros((8, BLOCK), F32)
        for r in range(0, g_sw, 8):
            beam = solar_col[r : r + 8, :] * cosine
            down_sw[r : r + 8, :] = beam
            top_beam = top_beam + beam
        flux[0:1, :] = jnp.zeros((1, BLOCK), F32)
        flux[1:2, :] = jnp.sum(top_beam, axis=0, keepdims=True)

    def enter_up(q):
        here, _ = place_of(q)
        albedo = albedo_ref[:, here]
        ground_beam = flux[1:2, :]
        gain[0:1, here] = (1.0 - albedo) * ground_beam
        up_lw[...] = jnp.zeros_like(up_lw)
        for r in range(0, g_sw, 8):
            up_sw[r : r + 8, :] = down_sw[r : r + 8, :] * albedo
        flux[2:3, :] = surface_ref[:, here] * total
        flux[3:4, :] = ground_beam * albedo

    def downward(q, out, early=None):
        here, first = place_of(q)
        half = lax.shift_right_logical(q, per_block.bit_length() - 1) & 1
        inverse = -LOG2E / cosine_ref[:, here]
        ready = levels if early is None else levels - EARLY
        extra = [ratio[pl.ds(first + n, 1), here] for n in range(ready, levels)]

        def absorbed(r, n):
            if n < ready:
                return out[r : r + 8, n * BLOCK : (n + 1) * BLOCK]
            return pre_buf[early, r : r + 8, (n - ready) * BLOCK : (n - ready + 1) * BLOCK] + extra[n - ready]

        diffuse, direct, step, own = [], [], [], []
        for n in range(levels):
            path_row = phys[pl.ds(LEV + first + n, 1), here]
            diffuse.append(path_row * DIFF)
            direct.append(path_row * inverse)
            own.append(planck_ext[pl.ds(first + n + 1, 1), here])
            step.append(planck_ext[pl.ds(first + n, 1), here] - own[-1])
        acc = [jnp.zeros((8, BLOCK), F32)] * levels
        for r in range(0, g_lw, 8):
            e = down_lw[r : r + 8, :]
            frac_here = frac_col[r : r + 8, :]
            for n in range(levels):
                t = jnp.exp2(absorbed(r, n) * diffuse[n])
                transmit[half, first + n, r : r + 8, :] = t
                e = t * (e + step[n])
                acc[n] = acc[n] + e * frac_here
            down_lw[r : r + 8, :] = e
        acc_sw = [jnp.zeros((8, BLOCK), F32)] * levels
        for r in range(0, g_sw, 8):
            b = down_sw[r : r + 8, :]
            for n in range(levels):
                x = absorbed(g_lw + r, n)
                transmit[half, first + n, g_lw + r : g_lw + r + 8, :] = jnp.exp2(x * diffuse[n])
                b = b * jnp.exp2(x * direct[n])
                acc_sw[n] = acc_sw[n] + b
            down_sw[r : r + 8, :] = b
        lw, sw = flux[0:1, :], flux[1:2, :]
        for n in range(levels):
            new_lw = jnp.sum(acc[n], axis=0, keepdims=True) + own[n] * total
            new_sw = jnp.sum(acc_sw[n], axis=0, keepdims=True)
            heat[pl.ds(first + n, 1), here] = lw - new_lw
            heat[pl.ds(LEV + first + n, 1), here] = sw - new_sw
            lw, sw = new_lw, new_sw
        flux[0:1, :] = lw
        flux[1:2, :] = sw

    def upward(q):
        here, first = place_of(q)
        half = lax.shift_right_logical(q, per_block.bit_length() - 1) & 1
        last = LEV - 1 - first
        step, own = [], []
        for n in range(levels):
            own.append(planck_ext[pl.ds(last - n + 1, 1), here])
            step.append(planck_ext[pl.ds(last - n + 2, 1), here] - own[-1])
        acc = [jnp.zeros((8, BLOCK), F32)] * levels
        for r in range(0, g_lw, 8):
            e = up_lw[r : r + 8, :]
            frac_here = frac_col[r : r + 8, :]
            for n in range(levels):
                e = transmit[half, last - n, r : r + 8, :] * (e + step[n])
                acc[n] = acc[n] + e * frac_here
            up_lw[r : r + 8, :] = e
        acc_sw = [jnp.zeros((8, BLOCK), F32)] * levels
        for r in range(0, g_sw, 8):
            v = up_sw[r : r + 8, :]
            for n in range(levels):
                v = transmit[half, last - n, g_lw + r : g_lw + r + 8, :] * v
                acc_sw[n] = acc_sw[n] + v
            up_sw[r : r + 8, :] = v
        lw, sw = flux[2:3, :], flux[3:4, :]
        for n in range(levels):
            new_lw = jnp.sum(acc[n], axis=0, keepdims=True) + own[n] * total
            new_sw = jnp.sum(acc_sw[n], axis=0, keepdims=True)
            row, row_sw = pl.ds(last - n, 1), pl.ds(LEV + last - n, 1)
            heat[row, here] = heat[row, here] + (lw - new_lw)
            heat[row_sw, here] = heat[row_sw, here] + (sw - new_sw)
            lw, sw = new_lw, new_sw
        flux[2:3, :] = lw
        flux[3:4, :] = sw

    groups = per_block * (columns // BLOCK)

    def fetch(i):
        return pltpu.make_async_copy(pre_ref.at[i], pre_buf.at[i & 1], pre_sem.at[i & 1])

    def turn(i):
        fetch(i).wait()

        @pl.when(i + 1 < groups // 2)
        def _():
            fetch(i + 1).start()

    def first_block(i, _):
        q = 2 * i
        turn(i)
        prepare(q + 1, mix_b, out_b, levels - EARLY)
        downward(q, out_a)
        prepare(q + 2, mix_a, out_a)
        downward(q + 1, out_b, i & 1)
        return 0

    def later_block(i, _):
        q = 2 * i
        turn(i)

        @pl.when((q & (per_block - 1)) == 0)
        def _():
            enter_up(q - per_block)
            enter_down(q)

        upward(q - per_block)
        prepare(q + 1, mix_b, out_b, levels - EARLY)
        downward(q, out_a)
        upward(q + 1 - per_block)
        prepare(jnp.minimum(q + 2, groups - 1), mix_a, out_a)
        downward(q + 1, out_b, i & 1)
        return 0

    def last_up(i, _):
        upward(i)
        return 0

    enter_down(0)
    prepare(0, mix_a, out_a)
    lax.fori_loop(0, per_block // 2, first_block, 0)
    lax.fori_loop(per_block // 2, groups // 2, later_block, 0)
    enter_up(groups - per_block)
    lax.fori_loop(groups - per_block, groups, last_up, 0)

    devices = slots // CAP
    half_rows = devices * CAP // 2
    sunlit = sunlit_ref[...]
    result = jnp.concatenate([heat[0:LEV, :], heat[LEV:, :] * sunlit.astype(F32)], axis=0)
    largest = jnp.max(jnp.abs(result), axis=1, keepdims=True)
    scale_code = jnp.ceil(jnp.log2(jnp.maximum(largest, 1e-30)) * 256.0 + 0.5)
    codes = result * (32767.0 * jnp.exp2(scale_code * (-1.0 / 256.0))) + 32768.5
    codes = jnp.clip(codes, 0.0, 65535.0).astype(I32)
    high = lax.shift_right_logical(codes, 8).astype(F32)
    low = (codes & 255).astype(F32)
    none = jnp.zeros_like(high)
    left = jnp.concatenate([high, none, low, none], axis=0).astype(BF16)
    right = jnp.concatenate([none, high, none, low], axis=0).astype(BF16)
    lanes = 4 * LEV
    diagonal = iota((2 * LEV, lanes), 0) == (iota((2 * LEV, lanes), 1) & (2 * LEV - 1))
    scale_row = jnp.sum(jnp.where(diagonal, scale_code, 0.0), axis=0, keepdims=True).astype(I32)

    sw_count = columns // 2
    sw_slot = slot_ref[...]
    owner = jnp.where(sunlit == 1, lax.shift_right_logical(sw_slot, sw_count.bit_length() - 1), owners)
    mark = jnp.where(iota((owners, columns), 0) == owner, 1.0, 0.0)
    place = owner * SW_CAP + dealt_rank(mark).astype(I32)
    scaled = gain[0:1, :] * (1.0 / GAIN_SCALE)
    first = jnp.floor(scaled * 32768.0)
    second = jnp.floor((scaled * 32768.0 - first) * 32768.0)
    first, second = first.astype(I32), second.astype(I32)
    own_slot = sw_slot & (sw_count - 1)
    pieces = [first, second, own_slot + 1]
    stack = jnp.zeros((16, columns), F32)
    at = iota((16, columns), 0)
    for n, x in enumerate(pieces):
        stack = jnp.where(at == 2 * n, lax.shift_right_logical(x, 8).astype(F32), stack)
        stack = jnp.where(at == 2 * n + 1, (x & 255).astype(F32), stack)
    stack = stack.astype(BF16)
    extras = []
    for o in range(0, owners, 2):
        pick = one_hot(iota((2 * SW_CAP, columns), 0) + o * SW_CAP, place)
        got = lax.dot_general(stack, pick, NT, preferred_element_type=F32)
        row_of = iota((8, lanes), 0)
        rows = [scale_row] + [
            (got[2 * n : 2 * n + 1] * 256.0 + got[2 * n + 1 : 2 * n + 2]).astype(I32) for n in range(3)
        ]
        both = jnp.zeros((8, lanes), I32)
        for n, x in enumerate(rows):
            both = jnp.where(row_of == n, x, both)
        extras += [both, both]
    extras = jnp.stack(extras)

    step = 256
    for k in range(half_rows // step):
        part = recv_ref[pl.ds(2 * k * step, 2 * step), :].astype(I32) + 32768
        label = jnp.broadcast_to(part[:, 3 * LEV : 3 * LEV + 1], (2 * step, 128)).reshape(2 * step // CAP, CAP, 128)
        got = jnp.zeros((step, 2 * lanes), F32)
        for side, value in enumerate((left, right)):
            mine = label[:, 8 * side : 8 * side + 8, :].reshape(step, 128)
            pick = jnp.concatenate(
                [one_hot(mine, iota((step, 128), 1) + c * 128) for c in range(columns // 128)], axis=1
            )
            got = got + lax.dot_general(pick, value, NT, preferred_element_type=F32)
        code = (got[:, :lanes] * 256.0 + got[:, lanes:]).astype(I32) - 32768
        code = code.reshape(step // 8, 8, lanes)
        more = jnp.concatenate([extras] * (step // 8 // owners), axis=0)
        out = jnp.concatenate([code, more], axis=1).reshape(2 * step, lanes)
        back_ref[pl.ds(2 * k * step, 2 * step), :] = out.astype(I16)


def home_kernel(back_ref, slot_ref, row_ref, lw_ref, sw_ref, surface_ref):
    columns = slot_ref.shape[1]
    slots = back_ref.shape[0]
    slot = slot_ref[...]
    got = jnp.zeros((4 * LEV, columns), F32)
    step = 256
    wide = 2 * LEV
    for k in range(slots // 2 // step):
        part = back_ref[pl.ds(2 * k * step, 2 * step), :].astype(I32).reshape(2 * step // CAP, CAP, 128)
        scale = jnp.exp2(part[:, 8:9, :].astype(F32) * (1.0 / 256.0)) * (1.0 / 32767.0)
        value = (part[:, :8, :].astype(F32) * scale).reshape(step, 128)
        first = value.astype(BF16)
        second = (value - first.astype(F32)).astype(BF16)
        row_of = iota((step, columns), 0) + k * step
        first_slot = lax.shift_right_logical(row_of, 3) * CAP + (row_of & 7)
        for side in range(2):
            pick = one_hot(first_slot + 8 * side, slot)
            lane = slice(side * wide, (side + 1) * wide)
            both = jnp.concatenate([first[:, lane], second[:, lane]], axis=1)
            got = got + lax.dot_general(both, pick, TN, preferred_element_type=F32)
    value = got[:wide] + got[wide:]
    lw_ref[...] = value[:LEV]
    sw_ref[...] = value[LEV:]

    count = surface_ref.shape[1]
    owners = 16
    mine = row_ref[0] * (owners * CAP)
    total = jnp.zeros((16, count), F32)
    odd = (row_ref[1] & 1) == 1
    for o in range(owners):
        got = back_ref[pl.ds(pl.multiple_of(mine + o * CAP, CAP), CAP), :].astype(I32)
        first, second, label = got[9:10], got[10:11], got[11:12]
        value = (first.astype(F32) + second.astype(F32) * (1.0 / 32768.0)) * (GAIN_SCALE / 32768.0)
        lane = iota((1, 128), 1)
        value = jnp.where((lane >= SW_CAP) == odd, value, 0.0)
        pick = one_hot(label - 1, iota((count, 128), 0))
        a, b, c = split3(value)
        at = iota((16, 128), 0)
        stack = jnp.where(
            at == 0, a.astype(F32), jnp.where(at == 1, b.astype(F32), jnp.where(at == 2, c.astype(F32), 0.0))
        )
        total = total + lax.dot_general(stack.astype(BF16), pick, NT, preferred_element_type=F32)
    surface_ref[...] = total[0:1] + total[1:2] + total[2:3]


def params():
    return pltpu.CompilerParams(vmem_limit_bytes=VMEM_LIMIT)


def vmem(count):
    return [pl.BlockSpec(memory_space=pltpu.VMEM)] * count


def body(
    planck_source,
    absorber_path,
    cloud_depth,
    span_map,
    surface_source,
    interp_index,
    interp_weight,
    sunlit,
    sw_slot,
    cos_zenith,
    albedo,
    table_lw,
    table_sw,
    planck_frac,
    solar_weight,
):
    columns = span_map.shape[0]
    owners = lax.axis_size("col")
    devices = lax.axis_size("dyn") * owners
    slots = devices * CAP
    g_lw, g_sw = table_lw.shape[0], table_sw.shape[0]

    def row(x):
        return x.reshape(1, -1)

    send, slot = pl.pallas_call(
        pack_kernel,
        out_shape=(jax.ShapeDtypeStruct((slots, 128), I16), jax.ShapeDtypeStruct((1, columns), I32)),
        in_specs=vmem(4),
        out_specs=tuple(vmem(2)),
        compiler_params=params(),
        name="pack",
    )(planck_source, absorber_path, cloud_depth, row(span_map))
    early_units = LEV // (2 * GROUP) * (columns // BLOCK)
    units = 4 // EARLY
    early = pl.pallas_call(
        absorb_kernel,
        grid=(early_units // units,),
        out_shape=jax.ShapeDtypeStruct((early_units, g_lw + g_sw, EARLY * BLOCK), F32),
        in_specs=vmem(4),
        out_specs=pl.BlockSpec((units, g_lw + g_sw, EARLY * BLOCK), lambda i: (i, 0, 0)),
        scratch_shapes=[
            pltpu.VMEM((4 * LEV, columns), F32),
            pltpu.VMEM((g_lw + g_sw, NTAB), BF16),
            pltpu.VMEM((NTAB, units * EARLY * BLOCK), BF16),
        ],
        compiler_params=params(),
        cost_estimate=pl.CostEstimate(
            flops=2 * (g_lw + g_sw) * NTAB * early_units * EARLY * BLOCK,
            bytes_accessed=4 * (g_lw + g_sw) * early_units * EARLY * BLOCK,
            transcendentals=0,
        ),
        name="absorb",
    )(interp_index, interp_weight, table_lw, table_sw)
    recv = lax.all_to_all(send.reshape(devices, CAP, 128), ("dyn", "col"), 0, 0, tiled=True)
    back = pl.pallas_call(
        partial(radiation_kernel, owners),
        out_shape=jax.ShapeDtypeStruct((slots, 128), I16),
        in_specs=vmem(1) + [pl.BlockSpec(memory_space=pl.ANY)] + vmem(11),
        out_specs=vmem(1)[0],
        scratch_shapes=[
            pltpu.VMEM((3 * LEV, columns), F32),
            pltpu.VMEM((4 * LEV, columns), F32),
            pltpu.VMEM((40, columns), F32),
            pltpu.VMEM((LEV, columns), F32),
            pltpu.VMEM((g_lw + g_sw, KPAD), BF16),
            pltpu.VMEM((KPAD, GROUP * BLOCK), BF16),
            pltpu.VMEM((KPAD, (GROUP - EARLY) * BLOCK), BF16),
            pltpu.VMEM((g_lw + g_sw, GROUP * BLOCK), F32),
            pltpu.VMEM((g_lw + g_sw, (GROUP - EARLY) * BLOCK), F32),
            pltpu.VMEM((2, LEV, g_lw + g_sw, BLOCK), F32),
            pltpu.VMEM((g_lw, BLOCK), F32),
            pltpu.VMEM((g_sw, BLOCK), F32),
            pltpu.VMEM((g_lw, BLOCK), F32),
            pltpu.VMEM((g_sw, BLOCK), F32),
            pltpu.VMEM((8, BLOCK), F32),
            pltpu.VMEM((g_lw, BLOCK), F32),
            pltpu.VMEM((g_sw, BLOCK), F32),
            pltpu.VMEM((2 * LEV, columns), F32),
            pltpu.VMEM((8, columns), F32),
            pltpu.VMEM((2, g_lw + g_sw, EARLY * BLOCK), F32),
            pltpu.SemaphoreType.DMA((2,)),
        ],
        compiler_params=params(),
        name="radiation",
    )(
        recv.reshape(slots, 128),
        early,
        row(surface_source),
        interp_index,
        interp_weight,
        row(sunlit),
        row(sw_slot),
        row(cos_zenith),
        row(albedo),
        table_lw,
        table_sw,
        row(planck_frac),
        row(solar_weight),
    )
    home = lax.all_to_all(back.reshape(devices, CAP, 128), ("dyn", "col"), 0, 0, tiled=True)
    place = jnp.stack([lax.axis_index("dyn"), lax.axis_index("col")]).astype(I32)
    heating_lw, heating_sw, surface = pl.pallas_call(
        home_kernel,
        out_shape=(jax.ShapeDtypeStruct((LEV, columns), F32),) * 2
        + (jax.ShapeDtypeStruct((1, columns // 2), F32),),
        in_specs=vmem(2) + [pl.BlockSpec(memory_space=pltpu.SMEM)],
        out_specs=tuple(vmem(3)),
        compiler_params=params(),
        name="home",
    )(home.reshape(slots, 128), slot, place)
    return (heating_lw, heating_sw, surface.reshape(-1))


def solution(mesh):
    columns = P(None, ("dyn", "col"))
    flat = P(("dyn", "col"))
    in_specs = (
        columns, columns, columns, flat, flat, columns, P(None, None, ("dyn", "col")),
        flat, flat, flat, flat, P(), P(), P(), P(),
    )
    out_specs = (columns, columns, flat)
    return jax.shard_map(body, mesh=mesh, in_specs=in_specs, out_specs=out_specs, check_vma=False)
```

```python
from functools import partial

import jax
import jax.numpy as jnp
from jax import lax
from jax.experimental import pallas as pl
from jax.experimental.pallas import tpu as pltpu
from jax.sharding import PartitionSpec as P

F32, BF16, I32, I16 = jnp.float32, jnp.bfloat16, jnp.int32, jnp.int16
TEMPS, PRESS, LEV = 14, 64, 32
NTAB = TEMPS * PRESS
KPAD = 1024
CAP = 16
SW_CAP = 64
LOG2E = 1.4426950408889634
DIFF = -1.66 * LOG2E
GAIN_SCALE = 8.0
CODES = ((0.5, 1.0), (0.2, 2.8), (0.0, 0.6))
BLOCK = 256
GROUP = 4
EARLY = 1
MIB = 1024 * 1024
NT = (((1,), (1,)), ((), ()))
TN = (((0,), (0,)), ((), ()))


def iota(shape, axis, dtype=I32):
    return lax.broadcasted_iota(dtype, shape, axis)


def one_hot(left, right):
    return jnp.where(left == right, 1.0, 0.0).astype(BF16)


def split3(x):
    a = x.astype(BF16)
    rest = x - a.astype(F32)
    b = rest.astype(BF16)
    c = (rest - b.astype(F32)).astype(BF16)
    return a, b, c


def dealt_rank(mark):
    parties, columns = mark.shape
    below = one_hot_less()
    before = jnp.zeros((parties, 1), F32)
    ranks = []
    for k in range(columns // 128):
        part = mark[:, k * 128 : (k + 1) * 128]
        running = jnp.dot(part.astype(BF16), below, preferred_element_type=F32) + before
        ranks.append(jnp.sum(running * part, axis=0, keepdims=True))
        before = before + jnp.sum(part, axis=1, keepdims=True)
    return jnp.concatenate(ranks, axis=1)


def one_hot_less():
    return jnp.where(iota((128, 128), 0) < iota((128, 128), 1), 1.0, 0.0).astype(BF16)


def mix_level(index, weight_rows, mix, lane):
    wide = index.shape[1]

    def spread(x):
        return jnp.broadcast_to(x.astype(F32).astype(BF16), (16, wide))

    temp = spread(lax.shift_right_logical(index, 6))
    press = spread(index & (PRESS - 1))
    after = press + jnp.asarray(1, BF16)
    w = [spread(x) for x in weight_rows]
    zero = jnp.zeros((16, wide), BF16)
    at = iota((16, wide), 0).astype(F32).astype(BF16)
    low, high = [], []
    for p in range(0, PRESS, 16):
        here = at + jnp.asarray(p, BF16)
        at0, at1 = here == press, here == after
        low.append(jnp.where(at0, w[0], jnp.where(at1, w[1], zero)))
        high.append(jnp.where(at0, w[2], jnp.where(at1, w[3], zero)))
    wrap = at == press - jnp.asarray(PRESS - 1, BF16)
    high[0] = jnp.where(wrap, w[1], high[0])
    over = jnp.where(wrap, w[3], zero)
    for t in range(TEMPS):
        is_temp = [temp == jnp.asarray(t - d, BF16) for d in range(3)]
        for n in range(PRESS // 16):
            tile = zero
            if n == 0 and t >= 2:
                tile = jnp.where(is_temp[2], over, tile)
            if t >= 1:
                tile = jnp.where(is_temp[1], high[n], tile)
            tile = jnp.where(is_temp[0], low[n], tile)
            first = t * PRESS + n * 16
            mix[first : first + 16, lane] = tile


def absorb_kernel(index_ref, weight_ref, table_lw_ref, table_sw_ref, out_ref, weights, table, mix):
    g_lw = table_lw_ref.shape[0]
    step = pl.program_id(0)

    @pl.when(step == 0)
    def _():
        for k in range(4):
            weights[pl.ds(k * LEV, LEV), :] = weight_ref[k].astype(F32)
        table[:g_lw, :] = table_lw_ref[...]
        table[g_lw:, :] = table_sw_ref[...]

    units = out_ref.shape[0]
    for u in range(units):
        unit = step * units + u
        per = LEV // (2 * GROUP)
        here = pl.ds(pl.multiple_of(unit // per * BLOCK, BLOCK), BLOCK)
        for n in range(EARLY):
            level = (unit % per) * 2 * GROUP + 2 * GROUP - EARLY + n
            row = pl.ds(level, 1)
            lane = slice((u * EARLY + n) * BLOCK, (u * EARLY + n + 1) * BLOCK)
            mix_level(index_ref[row, here], [weights[pl.ds(c * LEV + level, 1), here] for c in range(4)], mix, lane)
    got = jnp.dot(table[...], mix[...], preferred_element_type=F32)
    for u in range(units):
        out_ref[u] = got[:, u * EARLY * BLOCK : (u + 1) * EARLY * BLOCK]


def pack_kernel(planck_ref, path_ref, cloud_ref, map_ref, send_ref, slot_ref):
    columns = map_ref.shape[1]
    devices = send_ref.shape[0] // CAP
    span = map_ref[...]
    shift = columns.bit_length() - 1
    target = lax.shift_right_logical(span, shift)
    mark = jnp.where(iota((devices, columns), 0) == target, 1.0, 0.0)
    slot = target * CAP + dealt_rank(mark).astype(I32)
    slot_ref[...] = slot
    codes = []
    for ref, (low, width) in zip((planck_ref, path_ref, cloud_ref), CODES):
        scaled = (ref[...] - low) * (65535.0 / width) + 0.5
        codes.append(jnp.clip(scaled, 0.0, 65535.0).astype(I32))
    codes.append(jnp.broadcast_to(span & (columns - 1), (LEV, columns)))
    code = jnp.concatenate(codes, axis=0)
    high = lax.shift_right_logical(code, 8).astype(F32).astype(BF16)
    low = (code & 255).astype(F32).astype(BF16)
    both = jnp.concatenate([high, low], axis=0)
    rows = 512
    for k in range(send_ref.shape[0] // rows):
        pick = one_hot(iota((rows, columns), 0) + k * rows, slot)
        got = lax.dot_general(pick, both, NT, preferred_element_type=F32)
        width = 4 * LEV
        value = got[:, :width] * 256.0 + got[:, width:] - 32768.0
        send_ref[pl.ds(k * rows, rows), :] = value.astype(I32).astype(I16)


def radiation_kernel(
    owners,
    recv_ref,
    pre_ref,
    surface_ref,
    index_ref,
    weight_ref,
    sunlit_ref,
    slot_ref,
    cosine_ref,
    albedo_ref,
    table_lw_ref,
    table_sw_ref,
    frac_ref,
    solar_ref,
    back_ref,
    phys,
    weights,
    planck_ext,
    ratio,
    table,
    mix_a,
    mix_b,
    out_a,
    out_b,
    transmit,
    down_lw,
    down_sw,
    up_lw,
    up_sw,
    flux,
    frac_col,
    solar_col,
    heat,
    gain,
    pre_buf,
    pre_sem,
):
    columns = index_ref.shape[1]
    slots = recv_ref.shape[0]
    g_lw, g_sw = table_lw_ref.shape[0], table_sw_ref.shape[0]
    g_all = g_lw + g_sw
    first_fetch = pltpu.make_async_copy(pre_ref.at[0], pre_buf.at[0], pre_sem.at[0])
    first_fetch.start()
    code = recv_ref[...].astype(I32) + 32768
    both = jnp.concatenate(
        [lax.shift_right_logical(code, 8).astype(F32).astype(BF16), (code & 255).astype(F32).astype(BF16)], axis=1
    )
    label = code[:, 3 * LEV : 3 * LEV + 1] - 0
    for k in range(columns // BLOCK):
        pick = one_hot(label, iota((slots, BLOCK), 1) + k * BLOCK)
        got = lax.dot_general(both, pick, TN, preferred_element_type=F32)
        value = got[: 4 * LEV] * 256.0 + got[4 * LEV :]
        for n, (low, width) in enumerate(CODES):
            phys[pl.ds(n * LEV, LEV), pl.ds(k * BLOCK, BLOCK)] = value[n * LEV : (n + 1) * LEV] * (width / 65535.0) + low
    planck = phys[0:LEV, :]
    path = phys[LEV : 2 * LEV, :]
    cloud = phys[2 * LEV : 3 * LEV, :]
    planck_ext[0:1, :] = jnp.zeros((1, columns), F32)
    planck_ext[pl.ds(1, LEV), :] = planck
    planck_ext[pl.ds(LEV + 1, 1), :] = surface_ref[...]
    ratio[...] = cloud / path
    for k in range(4):
        weights[pl.ds(k * LEV, LEV), :] = weight_ref[k].astype(F32)
    ones = jnp.where(iota((g_all, 128), 1) < 3, 1.0, 0.0).astype(BF16)
    table[:g_lw, :NTAB] = table_lw_ref[...]
    table[g_lw:, :NTAB] = table_sw_ref[...]
    table[:, NTAB:] = ones
    for mix in (mix_a, mix_b):
        mix[NTAB:, :] = jnp.zeros((KPAD - NTAB, mix.shape[1]), BF16)
    frac = jnp.sum(jnp.where(iota((g_lw, g_lw), 0) == iota((g_lw, g_lw), 1), frac_ref[...], 0.0), axis=1, keepdims=True)
    solar = jnp.sum(jnp.where(iota((g_sw, g_sw), 0) == iota((g_sw, g_sw), 1), solar_ref[...], 0.0), axis=1, keepdims=True)
    frac_col[...] = jnp.broadcast_to(frac, frac_col.shape)
    solar_col[...] = jnp.broadcast_to(solar, solar_col.shape)
    total = jnp.sum(frac_ref[...])
    levels = GROUP
    per_block = LEV // levels
    width = levels * BLOCK

    def place_of(q):
        base = pl.multiple_of(lax.shift_right_logical(q, per_block.bit_length() - 1) * BLOCK, BLOCK)
        return pl.ds(base, BLOCK), (q & (per_block - 1)) * levels

    def prepare(q, mix, out, count=GROUP):
        here, first = place_of(q)
        for n in range(count):
            level = first + n
            row = pl.ds(level, 1)
            lane = slice(n * BLOCK, (n + 1) * BLOCK)
            mix_level(index_ref[row, here], [weights[pl.ds(c * LEV + level, 1), here] for c in range(4)], mix, lane)
            pieces = split3(ratio[row, here])
            tail = [jnp.broadcast_to(x.astype(F32), (16, BLOCK)) for x in pieces]
            which = iota((16, BLOCK), 0)
            mix[NTAB : NTAB + 16, lane] = jnp.where(
                which == 0, tail[0], jnp.where(which == 1, tail[1], jnp.where(which == 2, tail[2], 0.0))
            ).astype(BF16)
        out[...] = jnp.dot(table[...], mix[...], preferred_element_type=F32)

    def enter_down(q):
        here, _ = place_of(q)
        down_lw[...] = jnp.zeros_like(down_lw)
        cosine = cosine_ref[:, here]
        top_beam = jnp.zeros((8, BLOCK), F32)
        for r in range(0, g_sw, 8):
            beam = solar_col[r : r + 8, :] * cosine
            down_sw[r : r + 8, :] = beam
            top_beam = top_beam + beam
        flux[0:1, :] = jnp.zeros((1, BLOCK), F32)
        flux[1:2, :] = jnp.sum(top_beam, axis=0, keepdims=True)

    def enter_up(q):
        here, _ = place_of(q)
        albedo = albedo_ref[:, here]
        ground_beam = flux[1:2, :]
        gain[0:1, here] = (1.0 - albedo) * ground_beam
        up_lw[...] = jnp.zeros_like(up_lw)
        for r in range(0, g_sw, 8):
            up_sw[r : r + 8, :] = down_sw[r : r + 8, :] * albedo
        flux[2:3, :] = surface_ref[:, here] * total
        flux[3:4, :] = ground_beam * albedo

    def downward(q, out, early=None):
        here, first = place_of(q)
        half = lax.shift_right_logical(q, per_block.bit_length() - 1) & 1
        inverse = -LOG2E / cosine_ref[:, here]
        ready = levels if early is None else levels - EARLY
        extra = [ratio[pl.ds(first + n, 1), here] for n in range(ready, levels)]

        def absorbed(r, n):
            if n < ready:
                return out[r : r + 8, n * BLOCK : (n + 1) * BLOCK]
            return pre_buf[early, r : r + 8, (n - ready) * BLOCK : (n - ready + 1) * BLOCK] + extra[n - ready]

        diffuse, direct, step, own = [], [], [], []
        for n in range(levels):
            path_row = phys[pl.ds(LEV + first + n, 1), here]
            diffuse.append(path_row * DIFF)
            direct.append(path_row * inverse)
            own.append(planck_ext[pl.ds(first + n + 1, 1), here])
            step.append(planck_ext[pl.ds(first + n, 1), here] - own[-1])
        acc = [jnp.zeros((8, BLOCK), F32)] * levels
        for r in range(0, g_lw, 8):
            e = down_lw[r : r + 8, :]
            frac_here = frac_col[r : r + 8, :]
            for n in range(levels):
                t = jnp.exp2(absorbed(r, n) * diffuse[n])
                transmit[half, first + n, r : r + 8, :] = t
                e = t * (e + step[n])
                acc[n] = acc[n] + e * frac_here
            down_lw[r : r + 8, :] = e
        acc_sw = [jnp.zeros((8, BLOCK), F32)] * levels
        for r in range(0, g_sw, 8):
            b = down_sw[r : r + 8, :]
            for n in range(levels):
                x = absorbed(g_lw + r, n)
                transmit[half, first + n, g_lw + r : g_lw + r + 8, :] = jnp.exp2(x * diffuse[n])
                b = b * jnp.exp2(x * direct[n])
                acc_sw[n] = acc_sw[n] + b
            down_sw[r : r + 8, :] = b
        lw, sw = flux[0:1, :], flux[1:2, :]
        for n in range(levels):
            new_lw = jnp.sum(acc[n], axis=0, keepdims=True) + own[n] * total
            new_sw = jnp.sum(acc_sw[n], axis=0, keepdims=True)
            heat[pl.ds(first + n, 1), here] = lw - new_lw
            heat[pl.ds(LEV + first + n, 1), here] = sw - new_sw
            lw, sw = new_lw, new_sw
        flux[0:1, :] = lw
        flux[1:2, :] = sw

    def upward(q):
        here, first = place_of(q)
        half = lax.shift_right_logical(q, per_block.bit_length() - 1) & 1
        last = LEV - 1 - first
        step, own = [], []
        for n in range(levels):
            own.append(planck_ext[pl.ds(last - n + 1, 1), here])
            step.append(planck_ext[pl.ds(last - n + 2, 1), here] - own[-1])
        acc = [jnp.zeros((8, BLOCK), F32)] * levels
        for r in range(0, g_lw, 8):
            e = up_lw[r : r + 8, :]
            frac_here = frac_col[r : r + 8, :]
            for n in range(levels):
                e = transmit[half, last - n, r : r + 8, :] * (e + step[n])
                acc[n] = acc[n] + e * frac_here
            up_lw[r : r + 8, :] = e
        acc_sw = [jnp.zeros((8, BLOCK), F32)] * levels
        for r in range(0, g_sw, 8):
            v = up_sw[r : r + 8, :]
            for n in range(levels):
                v = transmit[half, last - n, g_lw + r : g_lw + r + 8, :] * v
                acc_sw[n] = acc_sw[n] + v
            up_sw[r : r + 8, :] = v
        lw, sw = flux[2:3, :], flux[3:4, :]
        for n in range(levels):
            new_lw = jnp.sum(acc[n], axis=0, keepdims=True) + own[n] * total
            new_sw = jnp.sum(acc_sw[n], axis=0, keepdims=True)
            row, row_sw = pl.ds(last - n, 1), pl.ds(LEV + last - n, 1)
            heat[row, here] = heat[row, here] + (lw - new_lw)
            heat[row_sw, here] = heat[row_sw, here] + (sw - new_sw)
            lw, sw = new_lw, new_sw
        flux[2:3, :] = lw
        flux[3:4, :] = sw

    groups = per_block * (columns // BLOCK)

    def fetch(i):
        return pltpu.make_async_copy(pre_ref.at[i], pre_buf.at[i & 1], pre_sem.at[i & 1])

    def turn(i):
        fetch(i).wait()

        @pl.when(i + 1 < groups // 2)
        def _():
            fetch(i + 1).start()

    def first_block(i, _):
        q = 2 * i
        turn(i)
        prepare(q + 1, mix_b, out_b, levels - EARLY)
        downward(q, out_a)
        prepare(q + 2, mix_a, out_a)
        downward(q + 1, out_b, i & 1)
        return 0

    def later_block(i, _):
        q = 2 * i
        turn(i)

        @pl.when((q & (per_block - 1)) == 0)
        def _():
            enter_up(q - per_block)
            enter_down(q)

        upward(q - per_block)
        prepare(q + 1, mix_b, out_b, levels - EARLY)
        downward(q, out_a)
        upward(q + 1 - per_block)
        prepare(jnp.minimum(q + 2, groups - 1), mix_a, out_a)
        downward(q + 1, out_b, i & 1)
        return 0

    def last_up(i, _):
        upward(i)
        return 0

    enter_down(0)
    prepare(0, mix_a, out_a)
    lax.fori_loop(0, per_block // 2, first_block, 0)
    lax.fori_loop(per_block // 2, groups // 2, later_block, 0)
    enter_up(groups - per_block)
    lax.fori_loop(groups - per_block, groups, last_up, 0)

    devices = slots // CAP
    half_rows = devices * CAP // 2
    sunlit = sunlit_ref[...]
    result = jnp.concatenate([heat[0:LEV, :], heat[LEV:, :] * sunlit.astype(F32)], axis=0)
    largest = jnp.max(jnp.abs(result), axis=1, keepdims=True)
    scale_code = jnp.ceil(jnp.log2(jnp.maximum(largest, 1e-30)) * 256.0 + 0.5)
    codes = result * (32767.0 * jnp.exp2(scale_code * (-1.0 / 256.0))) + 32768.5
    codes = jnp.clip(codes, 0.0, 65535.0).astype(I32)
    high = lax.shift_right_logical(codes, 8).astype(F32)
    low = (codes & 255).astype(F32)
    none = jnp.zeros_like(high)
    left = jnp.concatenate([high, none, low, none], axis=0).astype(BF16)
    right = jnp.concatenate([none, high, none, low], axis=0).astype(BF16)
    lanes = 4 * LEV
    diagonal = iota((2 * LEV, lanes), 0) == (iota((2 * LEV, lanes), 1) & (2 * LEV - 1))
    scale_row = jnp.sum(jnp.where(diagonal, scale_code, 0.0), axis=0, keepdims=True).astype(I32)

    sw_count = columns // 2
    sw_slot = slot_ref[...]
    owner = jnp.where(sunlit == 1, lax.shift_right_logical(sw_slot, sw_count.bit_length() - 1), owners)
    mark = jnp.where(iota((owners, columns), 0) == owner, 1.0, 0.0)
    place = owner * SW_CAP + dealt_rank(mark).astype(I32)
    scaled = gain[0:1, :] * (1.0 / GAIN_SCALE)
    first = jnp.floor(scaled * 32768.0)
    second = jnp.floor((scaled * 32768.0 - first) * 32768.0)
    first, second = first.astype(I32), second.astype(I32)
    own_slot = sw_slot & (sw_count - 1)
    pieces = [first, second, own_slot + 1]
    stack = jnp.zeros((16, columns), F32)
    at = iota((16, columns), 0)
    for n, x in enumerate(pieces):
        stack = jnp.where(at == 2 * n, lax.shift_right_logical(x, 8).astype(F32), stack)
        stack = jnp.where(at == 2 * n + 1, (x & 255).astype(F32), stack)
    stack = stack.astype(BF16)
    extras = []
    for o in range(0, owners, 2):
        pick = one_hot(iota((2 * SW_CAP, columns), 0) + o * SW_CAP, place)
        got = lax.dot_general(stack, pick, NT, preferred_element_type=F32)
        row_of = iota((8, lanes), 0)
        rows = [scale_row] + [
            (got[2 * n : 2 * n + 1] * 256.0 + got[2 * n + 1 : 2 * n + 2]).astype(I32) for n in range(3)
        ]
        both = jnp.zeros((8, lanes), I32)
        for n, x in enumerate(rows):
            both = jnp.where(row_of == n, x, both)
        extras += [both, both]
    extras = jnp.stack(extras)

    step = 256
    for k in range(half_rows // step):
        part = recv_ref[pl.ds(2 * k * step, 2 * step), :].astype(I32) + 32768
        label = jnp.broadcast_to(part[:, 3 * LEV : 3 * LEV + 1], (2 * step, 128)).reshape(2 * step // CAP, CAP, 128)
        got = jnp.zeros((step, 2 * lanes), F32)
        for side, value in enumerate((left, right)):
            mine = label[:, 8 * side : 8 * side + 8, :].reshape(step, 128)
            pick = jnp.concatenate(
                [one_hot(mine, iota((step, 128), 1) + c * 128) for c in range(columns // 128)], axis=1
            )
            got = got + lax.dot_general(pick, value, NT, preferred_element_type=F32)
        code = (got[:, :lanes] * 256.0 + got[:, lanes:]).astype(I32) - 32768
        code = code.reshape(step // 8, 8, lanes)
        more = jnp.concatenate([extras] * (step // 8 // owners), axis=0)
        out = jnp.concatenate([code, more], axis=1).reshape(2 * step, lanes)
        back_ref[pl.ds(2 * k * step, 2 * step), :] = out.astype(I16)


def home_kernel(back_ref, slot_ref, lw_ref, sw_ref, surface_ref):
    columns = slot_ref.shape[1]
    slots = back_ref.shape[0]
    slot = slot_ref[...]
    got = jnp.zeros((4 * LEV, columns), F32)
    step = 256
    wide = 2 * LEV
    for k in range(slots // 2 // step):
        part = back_ref[pl.ds(2 * k * step, 2 * step), :].astype(I32).reshape(2 * step // CAP, CAP, 128)
        scale = jnp.exp2(part[:, 8:9, :].astype(F32) * (1.0 / 256.0)) * (1.0 / 32767.0)
        value = (part[:, :8, :].astype(F32) * scale).reshape(step, 128)
        first = value.astype(BF16)
        second = (value - first.astype(F32)).astype(BF16)
        row_of = iota((step, columns), 0) + k * step
        first_slot = lax.shift_right_logical(row_of, 3) * CAP + (row_of & 7)
        for side in range(2):
            pick = one_hot(first_slot + 8 * side, slot)
            lane = slice(side * wide, (side + 1) * wide)
            both = jnp.concatenate([first[:, lane], second[:, lane]], axis=1)
            got = got + lax.dot_general(both, pick, TN, preferred_element_type=F32)
    value = got[:wide] + got[wide:]
    lw_ref[...] = value[:LEV]
    sw_ref[...] = value[LEV:]

    count = surface_ref.shape[1]
    owners = 16
    mine = lax.axis_index("dyn") * (owners * CAP)
    total = jnp.zeros((16, count), F32)
    odd = (lax.axis_index("col") & 1) == 1
    for o in range(owners):
        got = back_ref[pl.ds(pl.multiple_of(mine + o * CAP, CAP), CAP), :].astype(I32)
        first, second, label = got[9:10], got[10:11], got[11:12]
        value = (first.astype(F32) + second.astype(F32) * (1.0 / 32768.0)) * (GAIN_SCALE / 32768.0)
        lane = iota((1, 128), 1)
        value = jnp.where((lane >= SW_CAP) == odd, value, 0.0)
        pick = one_hot(label - 1, iota((count, 128), 0))
        a, b, c = split3(value)
        at = iota((16, 128), 0)
        stack = jnp.where(
            at == 0, a.astype(F32), jnp.where(at == 1, b.astype(F32), jnp.where(at == 2, c.astype(F32), 0.0))
        )
        total = total + lax.dot_general(stack.astype(BF16), pick, NT, preferred_element_type=F32)
    surface_ref[...] = total[0:1] + total[1:2] + total[2:3]


def params(mib):
    return pltpu.CompilerParams(vmem_limit_bytes=mib * MIB)


def vmem(count):
    return [pl.BlockSpec(memory_space=pltpu.VMEM)] * count


def body(
    planck_source,
    absorber_path,
    cloud_depth,
    span_map,
    surface_source,
    interp_index,
    interp_weight,
    sunlit,
    sw_slot,
    cos_zenith,
    albedo,
    table_lw,
    table_sw,
    planck_frac,
    solar_weight,
):
    columns = span_map.shape[0]
    owners = lax.axis_size("col")
    devices = lax.axis_size("dyn") * owners
    slots = devices * CAP
    g_lw, g_sw = table_lw.shape[0], table_sw.shape[0]

    def row(x):
        return x.reshape(1, -1)

    send, slot = pl.pallas_call(
        pack_kernel,
        out_shape=(jax.ShapeDtypeStruct((slots, 128), I16), jax.ShapeDtypeStruct((1, columns), I32)),
        in_specs=vmem(4),
        out_specs=tuple(vmem(2)),
        compiler_params=params(16),
        name="pack",
    )(planck_source, absorber_path, cloud_depth, row(span_map))
    early_units = LEV // (2 * GROUP) * (columns // BLOCK)
    units = 4 // EARLY
    early = pl.pallas_call(
        absorb_kernel,
        grid=(early_units // units,),
        out_shape=jax.ShapeDtypeStruct((early_units, g_lw + g_sw, EARLY * BLOCK), F32),
        in_specs=vmem(4),
        out_specs=pl.BlockSpec((units, g_lw + g_sw, EARLY * BLOCK), lambda i: (i, 0, 0)),
        scratch_shapes=[
            pltpu.VMEM((4 * LEV, columns), F32),
            pltpu.VMEM((g_lw + g_sw, NTAB), BF16),
            pltpu.VMEM((NTAB, units * EARLY * BLOCK), BF16),
        ],
        compiler_params=params(24),
        cost_estimate=pl.CostEstimate(
            flops=2 * (g_lw + g_sw) * NTAB * early_units * EARLY * BLOCK,
            bytes_accessed=4 * (g_lw + g_sw) * early_units * EARLY * BLOCK,
            transcendentals=0,
        ),
        name="absorb",
    )(interp_index, interp_weight, table_lw, table_sw)
    recv = lax.all_to_all(send.reshape(devices, CAP, 128), ("dyn", "col"), 0, 0, tiled=True)
    back = pl.pallas_call(
        partial(radiation_kernel, owners),
        out_shape=jax.ShapeDtypeStruct((slots, 128), I16),
        in_specs=vmem(1) + [pl.BlockSpec(memory_space=pl.ANY)] + vmem(11),
        out_specs=vmem(1)[0],
        scratch_shapes=[
            pltpu.VMEM((3 * LEV, columns), F32),
            pltpu.VMEM((4 * LEV, columns), F32),
            pltpu.VMEM((40, columns), F32),
            pltpu.VMEM((LEV, columns), F32),
            pltpu.VMEM((g_lw + g_sw, KPAD), BF16),
            pltpu.VMEM((KPAD, GROUP * BLOCK), BF16),
            pltpu.VMEM((KPAD, (GROUP - EARLY) * BLOCK), BF16),
            pltpu.VMEM((g_lw + g_sw, GROUP * BLOCK), F32),
            pltpu.VMEM((g_lw + g_sw, (GROUP - EARLY) * BLOCK), F32),
            pltpu.VMEM((2, LEV, g_lw + g_sw, BLOCK), F32),
            pltpu.VMEM((g_lw, BLOCK), F32),
            pltpu.VMEM((g_sw, BLOCK), F32),
            pltpu.VMEM((g_lw, BLOCK), F32),
            pltpu.VMEM((g_sw, BLOCK), F32),
            pltpu.VMEM((8, BLOCK), F32),
            pltpu.VMEM((g_lw, BLOCK), F32),
            pltpu.VMEM((g_sw, BLOCK), F32),
            pltpu.VMEM((2 * LEV, columns), F32),
            pltpu.VMEM((8, columns), F32),
            pltpu.VMEM((2, g_lw + g_sw, EARLY * BLOCK), F32),
            pltpu.SemaphoreType.DMA((2,)),
        ],
        compiler_params=params(48),
        name="radiation",
    )(
        recv.reshape(slots, 128),
        early,
        row(surface_source),
        interp_index,
        interp_weight,
        row(sunlit),
        row(sw_slot),
        row(cos_zenith),
        row(albedo),
        table_lw,
        table_sw,
        row(planck_frac),
        row(solar_weight),
    )
    home = lax.all_to_all(back.reshape(devices, CAP, 128), ("dyn", "col"), 0, 0, tiled=True)
    heating_lw, heating_sw, surface = pl.pallas_call(
        home_kernel,
        out_shape=(jax.ShapeDtypeStruct((LEV, columns), F32),) * 2
        + (jax.ShapeDtypeStruct((1, columns // 2), F32),),
        in_specs=vmem(2),
        out_specs=tuple(vmem(3)),
        compiler_params=params(16),
        name="home",
    )(home.reshape(slots, 128), slot)
    return (heating_lw, heating_sw, surface.reshape(-1))


def solution(mesh):
    columns = P(None, ("dyn", "col"))
    flat = P(("dyn", "col"))
    in_specs = (
        columns, columns, columns, flat, flat, columns, P(None, None, ("dyn", "col")),
        flat, flat, flat, flat, P(), P(), P(), P(),
    )
    out_specs = (columns, columns, flat)
    return jax.shard_map(body, mesh=mesh, in_specs=in_specs, out_specs=out_specs, check_vma=False)
```

```python
from functools import partial

import jax
import jax.numpy as jnp
from jax import lax
from jax.experimental import pallas as pl
from jax.experimental.pallas import tpu as pltpu
from jax.sharding import PartitionSpec as P

F32, BF16, I32, I16 = jnp.float32, jnp.bfloat16, jnp.int32, jnp.int16
TEMPS, PRESS, LEV = 14, 64, 32
NTAB = TEMPS * PRESS
KPAD = 1024
CAP = 16
SW_CAP = 64
LOG2E = 1.4426950408889634
DIFF = -1.66 * LOG2E
GAIN_SCALE = 8.0
CODES = ((0.5, 1.0), (0.2, 2.8), (0.0, 0.6))
BLOCK = 256
GROUP = 4
EARLY = 1
MIB = 1024 * 1024
NT = (((1,), (1,)), ((), ()))
TN = (((0,), (0,)), ((), ()))


def iota(shape, axis, dtype=I32):
    return lax.broadcasted_iota(dtype, shape, axis)


def one_hot(left, right):
    return jnp.where(left == right, 1.0, 0.0).astype(BF16)


def split3(x):
    a = x.astype(BF16)
    rest = x - a.astype(F32)
    b = rest.astype(BF16)
    c = (rest - b.astype(F32)).astype(BF16)
    return a, b, c


def dealt_rank(mark):
    parties, columns = mark.shape
    below = one_hot_less()
    before = jnp.zeros((parties, 1), F32)
    ranks = []
    for k in range(columns // 128):
        part = mark[:, k * 128 : (k + 1) * 128]
        running = jnp.dot(part.astype(BF16), below, preferred_element_type=F32) + before
        ranks.append(jnp.sum(running * part, axis=0, keepdims=True))
        before = before + jnp.sum(part, axis=1, keepdims=True)
    return jnp.concatenate(ranks, axis=1)


def one_hot_less():
    return jnp.where(iota((128, 128), 0) < iota((128, 128), 1), 1.0, 0.0).astype(BF16)


def mix_level(index, weight_rows, mix, lane):
    wide = index.shape[1]

    def spread(x):
        return jnp.broadcast_to(x.astype(F32).astype(BF16), (16, wide))

    temp = spread(lax.shift_right_logical(index, 6))
    press = spread(index & (PRESS - 1))
    after = press + jnp.asarray(1, BF16)
    w = [spread(x) for x in weight_rows]
    zero = jnp.zeros((16, wide), BF16)
    at = iota((16, wide), 0).astype(F32).astype(BF16)
    low, high = [], []
    for p in range(0, PRESS, 16):
        here = at + jnp.asarray(p, BF16)
        at0, at1 = here == press, here == after
        low.append(jnp.where(at0, w[0], jnp.where(at1, w[1], zero)))
        high.append(jnp.where(at0, w[2], jnp.where(at1, w[3], zero)))
    wrap = at == press - jnp.asarray(PRESS - 1, BF16)
    high[0] = jnp.where(wrap, w[1], high[0])
    over = jnp.where(wrap, w[3], zero)
    for t in range(TEMPS):
        is_temp = [temp == jnp.asarray(t - d, BF16) for d in range(3)]
        for n in range(PRESS // 16):
            tile = zero
            if n == 0 and t >= 2:
                tile = jnp.where(is_temp[2], over, tile)
            if t >= 1:
                tile = jnp.where(is_temp[1], high[n], tile)
            tile = jnp.where(is_temp[0], low[n], tile)
            first = t * PRESS + n * 16
            mix[first : first + 16, lane] = tile


def absorb_kernel(index_ref, weight_ref, table_lw_ref, table_sw_ref, out_ref, weights, table, mix):
    g_lw = table_lw_ref.shape[0]
    step = pl.program_id(0)

    @pl.when(step == 0)
    def _():
        for k in range(4):
            weights[pl.ds(k * LEV, LEV), :] = weight_ref[k].astype(F32)
        table[:g_lw, :] = table_lw_ref[...]
        table[g_lw:, :] = table_sw_ref[...]

    units = out_ref.shape[0]
    for u in range(units):
        unit = step * units + u
        per = LEV // (2 * GROUP)
        here = pl.ds(pl.multiple_of(unit // per * BLOCK, BLOCK), BLOCK)
        for n in range(EARLY):
            level = (unit % per) * 2 * GROUP + 2 * GROUP - EARLY + n
            row = pl.ds(level, 1)
            lane = slice((u * EARLY + n) * BLOCK, (u * EARLY + n + 1) * BLOCK)
            mix_level(index_ref[row, here], [weights[pl.ds(c * LEV + level, 1), here] for c in range(4)], mix, lane)
    got = jnp.dot(table[...], mix[...], preferred_element_type=F32)
    for u in range(units):
        out_ref[u] = got[:, u * EARLY * BLOCK : (u + 1) * EARLY * BLOCK]


def pack_kernel(planck_ref, path_ref, cloud_ref, map_ref, send_ref, slot_ref):
    columns = map_ref.shape[1]
    devices = send_ref.shape[0] // CAP
    span = map_ref[...]
    shift = columns.bit_length() - 1
    target = lax.shift_right_logical(span, shift)
    mark = jnp.where(iota((devices, columns), 0) == target, 1.0, 0.0)
    slot = target * CAP + dealt_rank(mark).astype(I32)
    slot_ref[...] = slot
    codes = []
    for ref, (low, width) in zip((planck_ref, path_ref, cloud_ref), CODES):
        scaled = (ref[...] - low) * (65535.0 / width) + 0.5
        codes.append(jnp.clip(scaled, 0.0, 65535.0).astype(I32))
    codes.append(jnp.broadcast_to(span & (columns - 1), (LEV, columns)))
    code = jnp.concatenate(codes, axis=0)
    high = lax.shift_right_logical(code, 8).astype(F32).astype(BF16)
    low = (code & 255).astype(F32).astype(BF16)
    both = jnp.concatenate([high, low], axis=0)
    rows = 512
    for k in range(send_ref.shape[0] // rows):
        pick = one_hot(iota((rows, columns), 0) + k * rows, slot)
        got = lax.dot_general(pick, both, NT, preferred_element_type=F32)
        width = 4 * LEV
        value = got[:, :width] * 256.0 + got[:, width:] - 32768.0
        send_ref[pl.ds(k * rows, rows), :] = value.astype(I32).astype(I16)


def radiation_kernel(
    owners,
    recv_ref,
    pre_ref,
    surface_ref,
    index_hbm,
    weight_hbm,
    sunlit_ref,
    slot_ref,
    cosine_ref,
    albedo_ref,
    table_lw_hbm,
    table_sw_hbm,
    frac_ref,
    solar_ref,
    back_ref,
    phys,
    weights,
    planck_ext,
    ratio,
    table,
    mix_a,
    mix_b,
    out_a,
    out_b,
    transmit,
    down_lw,
    down_sw,
    up_lw,
    up_sw,
    flux,
    frac_col,
    solar_col,
    heat,
    gain,
    pre_buf,
    index_ref,
    weight_ref,
    pre_sem,
    load_sem,
):
    columns = index_ref.shape[1]
    slots = recv_ref.shape[0]
    g_lw, g_sw = table_lw_hbm.shape[0], table_sw_hbm.shape[0]
    loads = [
        pltpu.make_async_copy(index_hbm, index_ref, load_sem.at[0]),
        pltpu.make_async_copy(weight_hbm, weight_ref, load_sem.at[1]),
        pltpu.make_async_copy(table_lw_hbm, table.at[pl.ds(0, g_lw), pl.ds(0, NTAB)], load_sem.at[2]),
        pltpu.make_async_copy(table_sw_hbm, table.at[pl.ds(g_lw, g_sw), pl.ds(0, NTAB)], load_sem.at[3]),
    ]
    for load in loads:
        load.start()
    g_all = g_lw + g_sw
    first_fetch = pltpu.make_async_copy(pre_ref.at[0], pre_buf.at[0], pre_sem.at[0])
    first_fetch.start()
    code = recv_ref[...].astype(I32) + 32768
    both = jnp.concatenate(
        [lax.shift_right_logical(code, 8).astype(F32).astype(BF16), (code & 255).astype(F32).astype(BF16)], axis=1
    )
    label = code[:, 3 * LEV : 3 * LEV + 1] - 0
    for k in range(columns // BLOCK):
        pick = one_hot(label, iota((slots, BLOCK), 1) + k * BLOCK)
        got = lax.dot_general(both, pick, TN, preferred_element_type=F32)
        value = got[: 4 * LEV] * 256.0 + got[4 * LEV :]
        for n, (low, width) in enumerate(CODES):
            phys[pl.ds(n * LEV, LEV), pl.ds(k * BLOCK, BLOCK)] = value[n * LEV : (n + 1) * LEV] * (width / 65535.0) + low
    planck = phys[0:LEV, :]
    path = phys[LEV : 2 * LEV, :]
    cloud = phys[2 * LEV : 3 * LEV, :]
    planck_ext[0:1, :] = jnp.zeros((1, columns), F32)
    planck_ext[pl.ds(1, LEV), :] = planck
    planck_ext[pl.ds(LEV + 1, 1), :] = surface_ref[...]
    ratio[...] = cloud / path
    for load in loads:
        load.wait()
    for k in range(4):
        weights[pl.ds(k * LEV, LEV), :] = weight_ref[k].astype(F32)
    ones = jnp.where(iota((g_all, 128), 1) < 3, 1.0, 0.0).astype(BF16)
    table[:, NTAB:] = ones
    for mix in (mix_a, mix_b):
        mix[NTAB:, :] = jnp.zeros((KPAD - NTAB, mix.shape[1]), BF16)
    frac = jnp.sum(jnp.where(iota((g_lw, g_lw), 0) == iota((g_lw, g_lw), 1), frac_ref[...], 0.0), axis=1, keepdims=True)
    solar = jnp.sum(jnp.where(iota((g_sw, g_sw), 0) == iota((g_sw, g_sw), 1), solar_ref[...], 0.0), axis=1, keepdims=True)
    frac_col[...] = jnp.broadcast_to(frac, frac_col.shape)
    solar_col[...] = jnp.broadcast_to(solar, solar_col.shape)
    total = jnp.sum(frac_ref[...])
    levels = GROUP
    per_block = LEV // levels
    width = levels * BLOCK

    def place_of(q):
        base = pl.multiple_of(lax.shift_right_logical(q, per_block.bit_length() - 1) * BLOCK, BLOCK)
        return pl.ds(base, BLOCK), (q & (per_block - 1)) * levels

    def prepare(q, mix, out, count=GROUP):
        here, first = place_of(q)
        for n in range(count):
            level = first + n
            row = pl.ds(level, 1)
            lane = slice(n * BLOCK, (n + 1) * BLOCK)
            mix_level(index_ref[row, here], [weights[pl.ds(c * LEV + level, 1), here] for c in range(4)], mix, lane)
            pieces = split3(ratio[row, here])
            tail = [jnp.broadcast_to(x.astype(F32), (16, BLOCK)) for x in pieces]
            which = iota((16, BLOCK), 0)
            mix[NTAB : NTAB + 16, lane] = jnp.where(
                which == 0, tail[0], jnp.where(which == 1, tail[1], jnp.where(which == 2, tail[2], 0.0))
            ).astype(BF16)
        out[...] = jnp.dot(table[...], mix[...], preferred_element_type=F32)

    def enter_down(q):
        here, _ = place_of(q)
        down_lw[...] = jnp.zeros_like(down_lw)
        cosine = cosine_ref[:, here]
        top_beam = jnp.zeros((8, BLOCK), F32)
        for r in range(0, g_sw, 8):
            beam = solar_col[r : r + 8, :] * cosine
            down_sw[r : r + 8, :] = beam
            top_beam = top_beam + beam
        flux[0:1, :] = jnp.zeros((1, BLOCK), F32)
        flux[1:2, :] = jnp.sum(top_beam, axis=0, keepdims=True)

    def enter_up(q):
        here, _ = place_of(q)
        albedo = albedo_ref[:, here]
        ground_beam = flux[1:2, :]
        gain[0:1, here] = (1.0 - albedo) * ground_beam
        up_lw[...] = jnp.zeros_like(up_lw)
        for r in range(0, g_sw, 8):
            up_sw[r : r + 8, :] = down_sw[r : r + 8, :] * albedo
        flux[2:3, :] = surface_ref[:, here] * total
        flux[3:4, :] = ground_beam * albedo

    def downward(q, out, early=None):
        here, first = place_of(q)
        half = lax.shift_right_logical(q, per_block.bit_length() - 1) & 1
        inverse = -LOG2E / cosine_ref[:, here]
        ready = levels if early is None else levels - EARLY
        extra = [ratio[pl.ds(first + n, 1), here] for n in range(ready, levels)]

        def absorbed(r, n):
            if n < ready:
                return out[r : r + 8, n * BLOCK : (n + 1) * BLOCK]
            return pre_buf[early, r : r + 8, (n - ready) * BLOCK : (n - ready + 1) * BLOCK] + extra[n - ready]

        diffuse, direct, step, own = [], [], [], []
        for n in range(levels):
            path_row = phys[pl.ds(LEV + first + n, 1), here]
            diffuse.append(path_row * DIFF)
            direct.append(path_row * inverse)
            own.append(planck_ext[pl.ds(first + n + 1, 1), here])
            step.append(planck_ext[pl.ds(first + n, 1), here] - own[-1])
        acc = [jnp.zeros((8, BLOCK), F32)] * levels
        for r in range(0, g_lw, 8):
            e = down_lw[r : r + 8, :]
            frac_here = frac_col[r : r + 8, :]
            for n in range(levels):
                t = jnp.exp2(absorbed(r, n) * diffuse[n])
                transmit[half, first + n, r : r + 8, :] = t
                e = t * (e + step[n])
                acc[n] = acc[n] + e * frac_here
            down_lw[r : r + 8, :] = e
        acc_sw = [jnp.zeros((8, BLOCK), F32)] * levels
        for r in range(0, g_sw, 8):
            b = down_sw[r : r + 8, :]
            for n in range(levels):
                x = absorbed(g_lw + r, n)
                transmit[half, first + n, g_lw + r : g_lw + r + 8, :] = jnp.exp2(x * diffuse[n])
                b = b * jnp.exp2(x * direct[n])
                acc_sw[n] = acc_sw[n] + b
            down_sw[r : r + 8, :] = b
        lw, sw = flux[0:1, :], flux[1:2, :]
        for n in range(levels):
            new_lw = jnp.sum(acc[n], axis=0, keepdims=True) + own[n] * total
            new_sw = jnp.sum(acc_sw[n], axis=0, keepdims=True)
            heat[pl.ds(first + n, 1), here] = lw - new_lw
            heat[pl.ds(LEV + first + n, 1), here] = sw - new_sw
            lw, sw = new_lw, new_sw
        flux[0:1, :] = lw
        flux[1:2, :] = sw

    def upward(q):
        here, first = place_of(q)
        half = lax.shift_right_logical(q, per_block.bit_length() - 1) & 1
        last = LEV - 1 - first
        step, own = [], []
        for n in range(levels):
            own.append(planck_ext[pl.ds(last - n + 1, 1), here])
            step.append(planck_ext[pl.ds(last - n + 2, 1), here] - own[-1])
        acc = [jnp.zeros((8, BLOCK), F32)] * levels
        for r in range(0, g_lw, 8):
            e = up_lw[r : r + 8, :]
            frac_here = frac_col[r : r + 8, :]
            for n in range(levels):
                e = transmit[half, last - n, r : r + 8, :] * (e + step[n])
                acc[n] = acc[n] + e * frac_here
            up_lw[r : r + 8, :] = e
        acc_sw = [jnp.zeros((8, BLOCK), F32)] * levels
        for r in range(0, g_sw, 8):
            v = up_sw[r : r + 8, :]
            for n in range(levels):
                v = transmit[half, last - n, g_lw + r : g_lw + r + 8, :] * v
                acc_sw[n] = acc_sw[n] + v
            up_sw[r : r + 8, :] = v
        lw, sw = flux[2:3, :], flux[3:4, :]
        for n in range(levels):
            new_lw = jnp.sum(acc[n], axis=0, keepdims=True) + own[n] * total
            new_sw = jnp.sum(acc_sw[n], axis=0, keepdims=True)
            row, row_sw = pl.ds(last - n, 1), pl.ds(LEV + last - n, 1)
            heat[row, here] = heat[row, here] + (lw - new_lw)
            heat[row_sw, here] = heat[row_sw, here] + (sw - new_sw)
            lw, sw = new_lw, new_sw
        flux[2:3, :] = lw
        flux[3:4, :] = sw

    groups = per_block * (columns // BLOCK)

    def fetch(i):
        return pltpu.make_async_copy(pre_ref.at[i], pre_buf.at[i & 1], pre_sem.at[i & 1])

    def turn(i):
        fetch(i).wait()

        @pl.when(i + 1 < groups // 2)
        def _():
            fetch(i + 1).start()

    def first_block(i, _):
        q = 2 * i
        turn(i)
        prepare(q + 1, mix_b, out_b, levels - EARLY)
        downward(q, out_a)
        prepare(q + 2, mix_a, out_a)
        downward(q + 1, out_b, i & 1)
        return 0

    def later_block(i, _):
        q = 2 * i
        turn(i)

        @pl.when((q & (per_block - 1)) == 0)
        def _():
            enter_up(q - per_block)
            enter_down(q)

        upward(q - per_block)
        upward(q + 1 - per_block)
        prepare(q + 1, mix_b, out_b, levels - EARLY)
        downward(q, out_a)
        prepare(jnp.minimum(q + 2, groups - 1), mix_a, out_a)
        downward(q + 1, out_b, i & 1)
        return 0

    def last_up(i, _):
        upward(i)
        return 0

    enter_down(0)
    prepare(0, mix_a, out_a)
    lax.fori_loop(0, per_block // 2, first_block, 0)
    lax.fori_loop(per_block // 2, groups // 2, later_block, 0)
    enter_up(groups - per_block)
    lax.fori_loop(groups - per_block, groups, last_up, 0)

    devices = slots // CAP
    half_rows = devices * CAP // 2
    sunlit = sunlit_ref[...]
    result = jnp.concatenate([heat[0:LEV, :], heat[LEV:, :] * sunlit.astype(F32)], axis=0)
    largest = jnp.max(jnp.abs(result), axis=1, keepdims=True)
    scale_code = jnp.ceil(jnp.log2(jnp.maximum(largest, 1e-30)) * 256.0 + 0.5)
    codes = result * (32767.0 * jnp.exp2(scale_code * (-1.0 / 256.0))) + 32768.5
    codes = jnp.clip(codes, 0.0, 65535.0).astype(I32)
    high = lax.shift_right_logical(codes, 8).astype(F32)
    low = (codes & 255).astype(F32)
    none = jnp.zeros_like(high)
    left = jnp.concatenate([high, none, low, none], axis=0).astype(BF16)
    right = jnp.concatenate([none, high, none, low], axis=0).astype(BF16)
    lanes = 4 * LEV
    diagonal = iota((2 * LEV, lanes), 0) == (iota((2 * LEV, lanes), 1) & (2 * LEV - 1))
    scale_row = jnp.sum(jnp.where(diagonal, scale_code, 0.0), axis=0, keepdims=True).astype(I32)

    sw_count = columns // 2
    sw_slot = slot_ref[...]
    owner = jnp.where(sunlit == 1, lax.shift_right_logical(sw_slot, sw_count.bit_length() - 1), owners)
    mark = jnp.where(iota((owners, columns), 0) == owner, 1.0, 0.0)
    place = owner * SW_CAP + dealt_rank(mark).astype(I32)
    scaled = gain[0:1, :] * (1.0 / GAIN_SCALE)
    first = jnp.floor(scaled * 32768.0)
    second = jnp.floor((scaled * 32768.0 - first) * 32768.0)
    first, second = first.astype(I32), second.astype(I32)
    own_slot = sw_slot & (sw_count - 1)
    pieces = [first, second, own_slot + 1]
    stack = jnp.zeros((16, columns), F32)
    at = iota((16, columns), 0)
    for n, x in enumerate(pieces):
        stack = jnp.where(at == 2 * n, lax.shift_right_logical(x, 8).astype(F32), stack)
        stack = jnp.where(at == 2 * n + 1, (x & 255).astype(F32), stack)
    stack = stack.astype(BF16)
    extras = []
    for o in range(0, owners, 2):
        pick = one_hot(iota((2 * SW_CAP, columns), 0) + o * SW_CAP, place)
        got = lax.dot_general(stack, pick, NT, preferred_element_type=F32)
        row_of = iota((8, lanes), 0)
        rows = [scale_row] + [
            (got[2 * n : 2 * n + 1] * 256.0 + got[2 * n + 1 : 2 * n + 2]).astype(I32) for n in range(3)
        ]
        both = jnp.zeros((8, lanes), I32)
        for n, x in enumerate(rows):
            both = jnp.where(row_of == n, x, both)
        extras += [both, both]
    extras = jnp.stack(extras)

    step = 256
    for k in range(half_rows // step):
        part = recv_ref[pl.ds(2 * k * step, 2 * step), :].astype(I32) + 32768
        label = jnp.broadcast_to(part[:, 3 * LEV : 3 * LEV + 1], (2 * step, 128)).reshape(2 * step // CAP, CAP, 128)
        got = jnp.zeros((step, 2 * lanes), F32)
        for side, value in enumerate((left, right)):
            mine = label[:, 8 * side : 8 * side + 8, :].reshape(step, 128)
            pick = jnp.concatenate(
                [one_hot(mine, iota((step, 128), 1) + c * 128) for c in range(columns // 128)], axis=1
            )
            got = got + lax.dot_general(pick, value, NT, preferred_element_type=F32)
        code = (got[:, :lanes] * 256.0 + got[:, lanes:]).astype(I32) - 32768
        code = code.reshape(step // 8, 8, lanes)
        more = jnp.concatenate([extras] * (step // 8 // owners), axis=0)
        out = jnp.concatenate([code, more], axis=1).reshape(2 * step, lanes)
        back_ref[pl.ds(2 * k * step, 2 * step), :] = out.astype(I16)


def home_kernel(back_ref, slot_ref, lw_ref, sw_ref, surface_ref):
    columns = slot_ref.shape[1]
    slots = back_ref.shape[0]
    slot = slot_ref[...]
    got = jnp.zeros((4 * LEV, columns), F32)
    step = 256
    wide = 2 * LEV
    for k in range(slots // 2 // step):
        part = back_ref[pl.ds(2 * k * step, 2 * step), :].astype(I32).reshape(2 * step // CAP, CAP, 128)
        scale = jnp.exp2(part[:, 8:9, :].astype(F32) * (1.0 / 256.0)) * (1.0 / 32767.0)
        value = (part[:, :8, :].astype(F32) * scale).reshape(step, 128)
        first = value.astype(BF16)
        second = (value - first.astype(F32)).astype(BF16)
        row_of = iota((step, columns), 0) + k * step
        first_slot = lax.shift_right_logical(row_of, 3) * CAP + (row_of & 7)
        for side in range(2):
            pick = one_hot(first_slot + 8 * side, slot)
            lane = slice(side * wide, (side + 1) * wide)
            both = jnp.concatenate([first[:, lane], second[:, lane]], axis=1)
            got = got + lax.dot_general(both, pick, TN, preferred_element_type=F32)
    value = got[:wide] + got[wide:]
    lw_ref[...] = value[:LEV]
    sw_ref[...] = value[LEV:]

    count = surface_ref.shape[1]
    owners = 16
    mine = lax.axis_index("dyn") * (owners * CAP)
    total = jnp.zeros((16, count), F32)
    odd = (lax.axis_index("col") & 1) == 1
    for o in range(owners):
        got = back_ref[pl.ds(pl.multiple_of(mine + o * CAP, CAP), CAP), :].astype(I32)
        first, second, label = got[9:10], got[10:11], got[11:12]
        value = (first.astype(F32) + second.astype(F32) * (1.0 / 32768.0)) * (GAIN_SCALE / 32768.0)
        lane = iota((1, 128), 1)
        value = jnp.where((lane >= SW_CAP) == odd, value, 0.0)
        pick = one_hot(label - 1, iota((count, 128), 0))
        a, b, c = split3(value)
        at = iota((16, 128), 0)
        stack = jnp.where(
            at == 0, a.astype(F32), jnp.where(at == 1, b.astype(F32), jnp.where(at == 2, c.astype(F32), 0.0))
        )
        total = total + lax.dot_general(stack.astype(BF16), pick, NT, preferred_element_type=F32)
    surface_ref[...] = total[0:1] + total[1:2] + total[2:3]


def params(mib):
    return pltpu.CompilerParams(vmem_limit_bytes=mib * MIB)


def hbm(count):
    return [pl.BlockSpec(memory_space=pltpu.HBM)] * count


def vmem(count):
    return [pl.BlockSpec(memory_space=pltpu.VMEM)] * count


def body(
    planck_source,
    absorber_path,
    cloud_depth,
    span_map,
    surface_source,
    interp_index,
    interp_weight,
    sunlit,
    sw_slot,
    cos_zenith,
    albedo,
    table_lw,
    table_sw,
    planck_frac,
    solar_weight,
):
    columns = span_map.shape[0]
    owners = lax.axis_size("col")
    devices = lax.axis_size("dyn") * owners
    slots = devices * CAP
    g_lw, g_sw = table_lw.shape[0], table_sw.shape[0]

    def row(x):
        return x.reshape(1, -1)

    send, slot = pl.pallas_call(
        pack_kernel,
        out_shape=(jax.ShapeDtypeStruct((slots, 128), I16), jax.ShapeDtypeStruct((1, columns), I32)),
        in_specs=vmem(4),
        out_specs=tuple(vmem(2)),
        compiler_params=params(60),
        name="pack",
    )(planck_source, absorber_path, cloud_depth, row(span_map))
    early_units = LEV // (2 * GROUP) * (columns // BLOCK)
    units = 4 // EARLY
    early = pl.pallas_call(
        absorb_kernel,
        grid=(early_units // units,),
        out_shape=jax.ShapeDtypeStruct((early_units, g_lw + g_sw, EARLY * BLOCK), F32),
        in_specs=vmem(4),
        out_specs=pl.BlockSpec((units, g_lw + g_sw, EARLY * BLOCK), lambda i: (i, 0, 0)),
        scratch_shapes=[
            pltpu.VMEM((4 * LEV, columns), F32),
            pltpu.VMEM((g_lw + g_sw, NTAB), BF16),
            pltpu.VMEM((NTAB, units * EARLY * BLOCK), BF16),
        ],
        compiler_params=params(60),
        cost_estimate=pl.CostEstimate(
            flops=2 * (g_lw + g_sw) * NTAB * early_units * EARLY * BLOCK,
            bytes_accessed=4 * (g_lw + g_sw) * early_units * EARLY * BLOCK,
            transcendentals=0,
        ),
        name="absorb",
    )(interp_index, interp_weight, table_lw, table_sw)
    recv = lax.all_to_all(send.reshape(devices, CAP, 128), ("dyn", "col"), 0, 0, tiled=True)
    back = pl.pallas_call(
        partial(radiation_kernel, owners),
        out_shape=jax.ShapeDtypeStruct((slots, 128), I16),
        in_specs=vmem(1) + hbm(1) + vmem(1) + hbm(2) + vmem(4) + hbm(2) + vmem(2),
        out_specs=vmem(1)[0],
        scratch_shapes=[
            pltpu.VMEM((3 * LEV, columns), F32),
            pltpu.VMEM((4 * LEV, columns), F32),
            pltpu.VMEM((40, columns), F32),
            pltpu.VMEM((LEV, columns), F32),
            pltpu.VMEM((g_lw + g_sw, KPAD), BF16),
            pltpu.VMEM((KPAD, GROUP * BLOCK), BF16),
            pltpu.VMEM((KPAD, (GROUP - EARLY) * BLOCK), BF16),
            pltpu.VMEM((g_lw + g_sw, GROUP * BLOCK), F32),
            pltpu.VMEM((g_lw + g_sw, (GROUP - EARLY) * BLOCK), F32),
            pltpu.VMEM((2, LEV, g_lw + g_sw, BLOCK), F32),
            pltpu.VMEM((g_lw, BLOCK), F32),
            pltpu.VMEM((g_sw, BLOCK), F32),
            pltpu.VMEM((g_lw, BLOCK), F32),
            pltpu.VMEM((g_sw, BLOCK), F32),
            pltpu.VMEM((8, BLOCK), F32),
            pltpu.VMEM((g_lw, BLOCK), F32),
            pltpu.VMEM((g_sw, BLOCK), F32),
            pltpu.VMEM((2 * LEV, columns), F32),
            pltpu.VMEM((8, columns), F32),
            pltpu.VMEM((2, g_lw + g_sw, EARLY * BLOCK), F32),
            pltpu.VMEM((LEV, columns), I32),
            pltpu.VMEM((4, LEV, columns), BF16),
            pltpu.SemaphoreType.DMA((2,)),
            pltpu.SemaphoreType.DMA((4,)),
        ],
        compiler_params=params(50),
        name="radiation",
    )(
        recv.reshape(slots, 128),
        early,
        row(surface_source),
        interp_index,
        interp_weight,
        row(sunlit),
        row(sw_slot),
        row(cos_zenith),
        row(albedo),
        table_lw,
        table_sw,
        row(planck_frac),
        row(solar_weight),
    )
    home = lax.all_to_all(back.reshape(devices, CAP, 128), ("dyn", "col"), 0, 0, tiled=True)
    heating_lw, heating_sw, surface = pl.pallas_call(
        home_kernel,
        out_shape=(jax.ShapeDtypeStruct((LEV, columns), F32),) * 2
        + (jax.ShapeDtypeStruct((1, columns // 2), F32),),
        in_specs=vmem(2),
        out_specs=tuple(vmem(3)),
        compiler_params=params(16),
        name="home",
    )(home.reshape(slots, 128), slot)
    return (heating_lw, heating_sw, surface.reshape(-1))


def solution(mesh):
    columns = P(None, ("dyn", "col"))
    flat = P(("dyn", "col"))
    in_specs = (
        columns, columns, columns, flat, flat, columns, P(None, None, ("dyn", "col")),
        flat, flat, flat, flat, P(), P(), P(), P(),
    )
    out_specs = (columns, columns, flat)
    return jax.shard_map(body, mesh=mesh, in_specs=in_specs, out_specs=out_specs, check_vma=False)
```

```python
from functools import partial

import jax
import jax.numpy as jnp
from jax import lax
from jax.experimental import pallas as pl
from jax.experimental.pallas import tpu as pltpu
from jax.sharding import PartitionSpec as P

F32, BF16, I32, I16 = jnp.float32, jnp.bfloat16, jnp.int32, jnp.int16
TEMPS, PRESS, LEV = 14, 64, 32
NTAB = TEMPS * PRESS
KPAD = 1024
CAP = 16
SW_CAP = 64
LOG2E = 1.4426950408889634
DIFF = -1.66 * LOG2E
GAIN_SCALE = 8.0
CODES = ((0.5, 1.0), (0.2, 2.8), (0.0, 0.6))
BLOCK = 256
GROUP = 4
EARLY = 1
MIB = 1024 * 1024
NT = (((1,), (1,)), ((), ()))
TN = (((0,), (0,)), ((), ()))


def iota(shape, axis, dtype=I32):
    return lax.broadcasted_iota(dtype, shape, axis)


def one_hot(left, right):
    return jnp.where(left == right, 1.0, 0.0).astype(BF16)


def split3(x):
    a = x.astype(BF16)
    rest = x - a.astype(F32)
    b = rest.astype(BF16)
    c = (rest - b.astype(F32)).astype(BF16)
    return a, b, c


def dealt_rank(mark):
    parties, columns = mark.shape
    below = one_hot_less()
    before = jnp.zeros((parties, 1), F32)
    ranks = []
    for k in range(columns // 128):
        part = mark[:, k * 128 : (k + 1) * 128]
        running = jnp.dot(part.astype(BF16), below, preferred_element_type=F32) + before
        ranks.append(jnp.sum(running * part, axis=0, keepdims=True))
        before = before + jnp.sum(part, axis=1, keepdims=True)
    return jnp.concatenate(ranks, axis=1)


def one_hot_less():
    return jnp.where(iota((128, 128), 0) < iota((128, 128), 1), 1.0, 0.0).astype(BF16)


def mix_level(index, weight_rows, mix, lane):
    wide = index.shape[1]

    def spread(x):
        return jnp.broadcast_to(x.astype(F32).astype(BF16), (16, wide))

    temp = spread(lax.shift_right_logical(index, 6))
    press = spread(index & (PRESS - 1))
    after = press + jnp.asarray(1, BF16)
    w = [spread(x) for x in weight_rows]
    zero = jnp.zeros((16, wide), BF16)
    at = iota((16, wide), 0).astype(F32).astype(BF16)
    low, high = [], []
    for p in range(0, PRESS, 16):
        here = at + jnp.asarray(p, BF16)
        at0, at1 = here == press, here == after
        low.append(jnp.where(at0, w[0], jnp.where(at1, w[1], zero)))
        high.append(jnp.where(at0, w[2], jnp.where(at1, w[3], zero)))
    wrap = at == press - jnp.asarray(PRESS - 1, BF16)
    high[0] = jnp.where(wrap, w[1], high[0])
    over = jnp.where(wrap, w[3], zero)
    for t in range(TEMPS):
        is_temp = [temp == jnp.asarray(t - d, BF16) for d in range(3)]
        for n in range(PRESS // 16):
            tile = zero
            if n == 0 and t >= 2:
                tile = jnp.where(is_temp[2], over, tile)
            if t >= 1:
                tile = jnp.where(is_temp[1], high[n], tile)
            tile = jnp.where(is_temp[0], low[n], tile)
            first = t * PRESS + n * 16
            mix[first : first + 16, lane] = tile


def absorb_kernel(index_ref, weight_ref, table_lw_ref, table_sw_ref, out_ref, weights, table, mix):
    g_lw = table_lw_ref.shape[0]
    step = pl.program_id(0)

    @pl.when(step == 0)
    def _():
        for k in range(4):
            weights[pl.ds(k * LEV, LEV), :] = weight_ref[k].astype(F32)
        table[:g_lw, :] = table_lw_ref[...]
        table[g_lw:, :] = table_sw_ref[...]

    units = out_ref.shape[0]
    for u in range(units):
        unit = step * units + u
        per = LEV // (2 * GROUP)
        here = pl.ds(pl.multiple_of(unit // per * BLOCK, BLOCK), BLOCK)
        for n in range(EARLY):
            level = (unit % per) * 2 * GROUP + 2 * GROUP - EARLY + n
            row = pl.ds(level, 1)
            lane = slice((u * EARLY + n) * BLOCK, (u * EARLY + n + 1) * BLOCK)
            mix_level(index_ref[row, here], [weights[pl.ds(c * LEV + level, 1), here] for c in range(4)], mix, lane)
    got = jnp.dot(table[...], mix[...], preferred_element_type=F32)
    for u in range(units):
        out_ref[u] = got[:, u * EARLY * BLOCK : (u + 1) * EARLY * BLOCK]


def pack_kernel(planck_ref, path_ref, cloud_ref, map_ref, send_ref, slot_ref):
    columns = map_ref.shape[1]
    devices = send_ref.shape[0] // CAP
    span = map_ref[...]
    shift = columns.bit_length() - 1
    target = lax.shift_right_logical(span, shift)
    mark = jnp.where(iota((devices, columns), 0) == target, 1.0, 0.0)
    slot = target * CAP + dealt_rank(mark).astype(I32)
    slot_ref[...] = slot
    codes = []
    for ref, (low, width) in zip((planck_ref, path_ref, cloud_ref), CODES):
        scaled = (ref[...] - low) * (65535.0 / width) + 0.5
        codes.append(jnp.clip(scaled, 0.0, 65535.0).astype(I32))
    codes.append(jnp.broadcast_to(span & (columns - 1), (LEV, columns)))
    code = jnp.concatenate(codes, axis=0)
    high = lax.shift_right_logical(code, 8).astype(F32).astype(BF16)
    low = (code & 255).astype(F32).astype(BF16)
    both = jnp.concatenate([high, low], axis=0)
    rows = 512
    for k in range(send_ref.shape[0] // rows):
        pick = one_hot(iota((rows, columns), 0) + k * rows, slot)
        got = lax.dot_general(pick, both, NT, preferred_element_type=F32)
        width = 4 * LEV
        value = got[:, :width] * 256.0 + got[:, width:] - 32768.0
        send_ref[pl.ds(k * rows, rows), :] = value.astype(I32).astype(I16)


def radiation_kernel(
    owners,
    recv_ref,
    pre_ref,
    surface_ref,
    index_ref,
    weight_ref,
    sunlit_ref,
    slot_ref,
    cosine_ref,
    albedo_ref,
    table_lw_ref,
    table_sw_ref,
    frac_ref,
    solar_ref,
    back_ref,
    phys,
    weights,
    planck_ext,
    ratio,
    table,
    mix_a,
    mix_b,
    out_a,
    out_b,
    transmit,
    down_lw,
    down_sw,
    up_lw,
    up_sw,
    flux,
    frac_col,
    solar_col,
    heat,
    gain,
    pre_buf,
    pre_sem,
):
    columns = index_ref.shape[1]
    slots = recv_ref.shape[0]
    g_lw, g_sw = table_lw_ref.shape[0], table_sw_ref.shape[0]
    g_all = g_lw + g_sw
    first_fetch = pltpu.make_async_copy(pre_ref.at[0], pre_buf.at[0], pre_sem.at[0])
    first_fetch.start()
    code = recv_ref[...].astype(I32) + 32768
    both = jnp.concatenate(
        [lax.shift_right_logical(code, 8).astype(F32).astype(BF16), (code & 255).astype(F32).astype(BF16)], axis=1
    )
    label = code[:, 3 * LEV : 3 * LEV + 1] - 0
    for k in range(columns // BLOCK):
        pick = one_hot(label, iota((slots, BLOCK), 1) + k * BLOCK)
        got = lax.dot_general(both, pick, TN, preferred_element_type=F32)
        value = got[: 4 * LEV] * 256.0 + got[4 * LEV :]
        for n, (low, width) in enumerate(CODES):
            phys[pl.ds(n * LEV, LEV), pl.ds(k * BLOCK, BLOCK)] = value[n * LEV : (n + 1) * LEV] * (width / 65535.0) + low
    planck = phys[0:LEV, :]
    path = phys[LEV : 2 * LEV, :]
    cloud = phys[2 * LEV : 3 * LEV, :]
    planck_ext[0:1, :] = jnp.zeros((1, columns), F32)
    planck_ext[pl.ds(1, LEV), :] = planck
    planck_ext[pl.ds(LEV + 1, 1), :] = surface_ref[...]
    ratio[...] = cloud / path
    for k in range(4):
        weights[pl.ds(k * LEV, LEV), :] = weight_ref[k].astype(F32)
    ones = jnp.where(iota((g_all, 128), 1) < 3, 1.0, 0.0).astype(BF16)
    table[:g_lw, :NTAB] = table_lw_ref[...]
    table[g_lw:, :NTAB] = table_sw_ref[...]
    table[:, NTAB:] = ones
    for mix in (mix_a, mix_b):
        mix[NTAB:, :] = jnp.zeros((KPAD - NTAB, mix.shape[1]), BF16)
    frac = jnp.sum(jnp.where(iota((g_lw, g_lw), 0) == iota((g_lw, g_lw), 1), frac_ref[...], 0.0), axis=1, keepdims=True)
    solar = jnp.sum(jnp.where(iota((g_sw, g_sw), 0) == iota((g_sw, g_sw), 1), solar_ref[...], 0.0), axis=1, keepdims=True)
    frac_col[...] = jnp.broadcast_to(frac, frac_col.shape)
    solar_col[...] = jnp.broadcast_to(solar, solar_col.shape)
    total = jnp.sum(frac_ref[...])
    levels = GROUP
    per_block = LEV // levels
    width = levels * BLOCK

    def place_of(q):
        base = pl.multiple_of(lax.shift_right_logical(q, per_block.bit_length() - 1) * BLOCK, BLOCK)
        return pl.ds(base, BLOCK), (q & (per_block - 1)) * levels

    def prepare(q, mix, out, count=GROUP):
        here, first = place_of(q)
        for n in range(count):
            level = first + n
            row = pl.ds(level, 1)
            lane = slice(n * BLOCK, (n + 1) * BLOCK)
            mix_level(index_ref[row, here], [weights[pl.ds(c * LEV + level, 1), here] for c in range(4)], mix, lane)
            pieces = split3(ratio[row, here])
            tail = [jnp.broadcast_to(x.astype(F32), (16, BLOCK)) for x in pieces]
            which = iota((16, BLOCK), 0)
            mix[NTAB : NTAB + 16, lane] = jnp.where(
                which == 0, tail[0], jnp.where(which == 1, tail[1], jnp.where(which == 2, tail[2], 0.0))
            ).astype(BF16)
        out[...] = jnp.dot(table[...], mix[...], preferred_element_type=F32)

    def enter_down(q):
        here, _ = place_of(q)
        down_lw[...] = jnp.zeros_like(down_lw)
        cosine = cosine_ref[:, here]
        top_beam = jnp.zeros((8, BLOCK), F32)
        for r in range(0, g_sw, 8):
            beam = solar_col[r : r + 8, :] * cosine
            down_sw[r : r + 8, :] = beam
            top_beam = top_beam + beam
        flux[0:1, :] = jnp.zeros((1, BLOCK), F32)
        flux[1:2, :] = jnp.sum(top_beam, axis=0, keepdims=True)

    def enter_up(q):
        here, _ = place_of(q)
        albedo = albedo_ref[:, here]
        ground_beam = flux[1:2, :]
        gain[0:1, here] = (1.0 - albedo) * ground_beam
        up_lw[...] = jnp.zeros_like(up_lw)
        for r in range(0, g_sw, 8):
            up_sw[r : r + 8, :] = down_sw[r : r + 8, :] * albedo
        flux[2:3, :] = surface_ref[:, here] * total
        flux[3:4, :] = ground_beam * albedo

    def downward(q, out, early=None):
        here, first = place_of(q)
        half = lax.shift_right_logical(q, per_block.bit_length() - 1) & 1
        inverse = -LOG2E / cosine_ref[:, here]
        ready = levels if early is None else levels - EARLY
        extra = [ratio[pl.ds(first + n, 1), here] for n in range(ready, levels)]

        def absorbed(r, n):
            if n < ready:
                return out[r : r + 8, n * BLOCK : (n + 1) * BLOCK]
            return pre_buf[early, r : r + 8, (n - ready) * BLOCK : (n - ready + 1) * BLOCK] + extra[n - ready]

        diffuse, direct, step, own = [], [], [], []
        for n in range(levels):
            path_row = phys[pl.ds(LEV + first + n, 1), here]
            diffuse.append(path_row * DIFF)
            direct.append(path_row * inverse)
            own.append(planck_ext[pl.ds(first + n + 1, 1), here])
            step.append(planck_ext[pl.ds(first + n, 1), here] - own[-1])
        acc = [jnp.zeros((8, BLOCK), F32)] * levels
        for r in range(0, g_lw, 8):
            e = down_lw[r : r + 8, :]
            frac_here = frac_col[r : r + 8, :]
            for n in range(levels):
                t = jnp.exp2(absorbed(r, n) * diffuse[n])
                transmit[half, first + n, r : r + 8, :] = t
                e = t * (e + step[n])
                acc[n] = acc[n] + e * frac_here
            down_lw[r : r + 8, :] = e
        acc_sw = [jnp.zeros((8, BLOCK), F32)] * levels
        for r in range(0, g_sw, 8):
            b = down_sw[r : r + 8, :]
            for n in range(levels):
                x = absorbed(g_lw + r, n)
                transmit[half, first + n, g_lw + r : g_lw + r + 8, :] = jnp.exp2(x * diffuse[n])
                b = b * jnp.exp2(x * direct[n])
                acc_sw[n] = acc_sw[n] + b
            down_sw[r : r + 8, :] = b
        lw, sw = flux[0:1, :], flux[1:2, :]
        for n in range(levels):
            new_lw = jnp.sum(acc[n], axis=0, keepdims=True) + own[n] * total
            new_sw = jnp.sum(acc_sw[n], axis=0, keepdims=True)
            heat[pl.ds(first + n, 1), here] = lw - new_lw
            heat[pl.ds(LEV + first + n, 1), here] = sw - new_sw
            lw, sw = new_lw, new_sw
        flux[0:1, :] = lw
        flux[1:2, :] = sw

    def upward(q):
        here, first = place_of(q)
        half = lax.shift_right_logical(q, per_block.bit_length() - 1) & 1
        last = LEV - 1 - first
        step, own = [], []
        for n in range(levels):
            own.append(planck_ext[pl.ds(last - n + 1, 1), here])
            step.append(planck_ext[pl.ds(last - n + 2, 1), here] - own[-1])
        acc = [jnp.zeros((8, BLOCK), F32)] * levels
        for r in range(0, g_lw, 8):
            e = up_lw[r : r + 8, :]
            frac_here = frac_col[r : r + 8, :]
            for n in range(levels):
                e = transmit[half, last - n, r : r + 8, :] * (e + step[n])
                acc[n] = acc[n] + e * frac_here
            up_lw[r : r + 8, :] = e
        acc_sw = [jnp.zeros((8, BLOCK), F32)] * levels
        for r in range(0, g_sw, 8):
            v = up_sw[r : r + 8, :]
            for n in range(levels):
                v = transmit[half, last - n, g_lw + r : g_lw + r + 8, :] * v
                acc_sw[n] = acc_sw[n] + v
            up_sw[r : r + 8, :] = v
        lw, sw = flux[2:3, :], flux[3:4, :]
        for n in range(levels):
            new_lw = jnp.sum(acc[n], axis=0, keepdims=True) + own[n] * total
            new_sw = jnp.sum(acc_sw[n], axis=0, keepdims=True)
            row, row_sw = pl.ds(last - n, 1), pl.ds(LEV + last - n, 1)
            heat[row, here] = heat[row, here] + (lw - new_lw)
            heat[row_sw, here] = heat[row_sw, here] + (sw - new_sw)
            lw, sw = new_lw, new_sw
        flux[2:3, :] = lw
        flux[3:4, :] = sw

    groups = per_block * (columns // BLOCK)

    def fetch(i):
        return pltpu.make_async_copy(pre_ref.at[i], pre_buf.at[i & 1], pre_sem.at[i & 1])

    def turn(i):
        fetch(i).wait()

        @pl.when(i + 1 < groups // 2)
        def _():
            fetch(i + 1).start()

    def first_block(i, _):
        q = 2 * i
        turn(i)
        prepare(q + 1, mix_b, out_b, levels - EARLY)
        downward(q, out_a)
        prepare(q + 2, mix_a, out_a)
        downward(q + 1, out_b, i & 1)
        return 0

    def later_block(i, _):
        q = 2 * i
        turn(i)

        @pl.when((q & (per_block - 1)) == 0)
        def _():
            enter_up(q - per_block)
            enter_down(q)

        upward(q - per_block)
        upward(q + 1 - per_block)
        prepare(q + 1, mix_b, out_b, levels - EARLY)
        downward(q, out_a)
        prepare(jnp.minimum(q + 2, groups - 1), mix_a, out_a)
        downward(q + 1, out_b, i & 1)
        return 0

    def last_up(i, _):
        upward(i)
        return 0

    enter_down(0)
    prepare(0, mix_a, out_a)
    lax.fori_loop(0, per_block // 2, first_block, 0)
    lax.fori_loop(per_block // 2, groups // 2, later_block, 0)
    enter_up(groups - per_block)
    lax.fori_loop(groups - per_block, groups, last_up, 0)

    devices = slots // CAP
    half_rows = devices * CAP // 2
    sunlit = sunlit_ref[...]
    result = jnp.concatenate([heat[0:LEV, :], heat[LEV:, :] * sunlit.astype(F32)], axis=0)
    largest = jnp.max(jnp.abs(result), axis=1, keepdims=True)
    scale_code = jnp.ceil(jnp.log2(jnp.maximum(largest, 1e-30)) * 256.0 + 0.5)
    codes = result * (32767.0 * jnp.exp2(scale_code * (-1.0 / 256.0))) + 32768.5
    codes = jnp.clip(codes, 0.0, 65535.0).astype(I32)
    high = lax.shift_right_logical(codes, 8).astype(F32)
    low = (codes & 255).astype(F32)
    none = jnp.zeros_like(high)
    left = jnp.concatenate([high, none, low, none], axis=0).astype(BF16)
    right = jnp.concatenate([none, high, none, low], axis=0).astype(BF16)
    lanes = 4 * LEV
    diagonal = iota((2 * LEV, lanes), 0) == (iota((2 * LEV, lanes), 1) & (2 * LEV - 1))
    scale_row = jnp.sum(jnp.where(diagonal, scale_code, 0.0), axis=0, keepdims=True).astype(I32)

    sw_count = columns // 2
    sw_slot = slot_ref[...]
    owner = jnp.where(sunlit == 1, lax.shift_right_logical(sw_slot, sw_count.bit_length() - 1), owners)
    mark = jnp.where(iota((owners, columns), 0) == owner, 1.0, 0.0)
    place = owner * SW_CAP + dealt_rank(mark).astype(I32)
    scaled = gain[0:1, :] * (1.0 / GAIN_SCALE)
    first = jnp.floor(scaled * 32768.0)
    second = jnp.floor((scaled * 32768.0 - first) * 32768.0)
    first, second = first.astype(I32), second.astype(I32)
    own_slot = sw_slot & (sw_count - 1)
    pieces = [first, second, own_slot + 1]
    stack = jnp.zeros((16, columns), F32)
    at = iota((16, columns), 0)
    for n, x in enumerate(pieces):
        stack = jnp.where(at == 2 * n, lax.shift_right_logical(x, 8).astype(F32), stack)
        stack = jnp.where(at == 2 * n + 1, (x & 255).astype(F32), stack)
    stack = stack.astype(BF16)
    extras = []
    for o in range(0, owners, 2):
        pick = one_hot(iota((2 * SW_CAP, columns), 0) + o * SW_CAP, place)
        got = lax.dot_general(stack, pick, NT, preferred_element_type=F32)
        row_of = iota((8, lanes), 0)
        rows = [scale_row] + [
            (got[2 * n : 2 * n + 1] * 256.0 + got[2 * n + 1 : 2 * n + 2]).astype(I32) for n in range(3)
        ]
        both = jnp.zeros((8, lanes), I32)
        for n, x in enumerate(rows):
            both = jnp.where(row_of == n, x, both)
        extras += [both, both]
    extras = jnp.stack(extras)

    step = 256
    for k in range(half_rows // step):
        part = recv_ref[pl.ds(2 * k * step, 2 * step), :].astype(I32) + 32768
        label = jnp.broadcast_to(part[:, 3 * LEV : 3 * LEV + 1], (2 * step, 128)).reshape(2 * step // CAP, CAP, 128)
        got = jnp.zeros((step, 2 * lanes), F32)
        for side, value in enumerate((left, right)):
            mine = label[:, 8 * side : 8 * side + 8, :].reshape(step, 128)
            pick = jnp.concatenate(
                [one_hot(mine, iota((step, 128), 1) + c * 128) for c in range(columns // 128)], axis=1
            )
            got = got + lax.dot_general(pick, value, NT, preferred_element_type=F32)
        code = (got[:, :lanes] * 256.0 + got[:, lanes:]).astype(I32) - 32768
        code = code.reshape(step // 8, 8, lanes)
        more = jnp.concatenate([extras] * (step // 8 // owners), axis=0)
        out = jnp.concatenate([code, more], axis=1).reshape(2 * step, lanes)
        back_ref[pl.ds(2 * k * step, 2 * step), :] = out.astype(I16)


def home_kernel(back_ref, slot_ref, lw_ref, sw_ref, surface_ref):
    columns = slot_ref.shape[1]
    slots = back_ref.shape[0]
    slot = slot_ref[...]
    got = jnp.zeros((4 * LEV, columns), F32)
    step = 256
    wide = 2 * LEV
    for k in range(slots // 2 // step):
        part = back_ref[pl.ds(2 * k * step, 2 * step), :].astype(I32).reshape(2 * step // CAP, CAP, 128)
        scale = jnp.exp2(part[:, 8:9, :].astype(F32) * (1.0 / 256.0)) * (1.0 / 32767.0)
        value = (part[:, :8, :].astype(F32) * scale).reshape(step, 128)
        first = value.astype(BF16)
        second = (value - first.astype(F32)).astype(BF16)
        row_of = iota((step, columns), 0) + k * step
        first_slot = lax.shift_right_logical(row_of, 3) * CAP + (row_of & 7)
        for side in range(2):
            pick = one_hot(first_slot + 8 * side, slot)
            lane = slice(side * wide, (side + 1) * wide)
            both = jnp.concatenate([first[:, lane], second[:, lane]], axis=1)
            got = got + lax.dot_general(both, pick, TN, preferred_element_type=F32)
    value = got[:wide] + got[wide:]
    lw_ref[...] = value[:LEV]
    sw_ref[...] = value[LEV:]

    count = surface_ref.shape[1]
    owners = 16
    mine = lax.axis_index("dyn") * (owners * CAP)
    total = jnp.zeros((16, count), F32)
    odd = (lax.axis_index("col") & 1) == 1
    for o in range(owners):
        got = back_ref[pl.ds(pl.multiple_of(mine + o * CAP, CAP), CAP), :].astype(I32)
        first, second, label = got[9:10], got[10:11], got[11:12]
        value = (first.astype(F32) + second.astype(F32) * (1.0 / 32768.0)) * (GAIN_SCALE / 32768.0)
        lane = iota((1, 128), 1)
        value = jnp.where((lane >= SW_CAP) == odd, value, 0.0)
        pick = one_hot(label - 1, iota((count, 128), 0))
        a, b, c = split3(value)
        at = iota((16, 128), 0)
        stack = jnp.where(
            at == 0, a.astype(F32), jnp.where(at == 1, b.astype(F32), jnp.where(at == 2, c.astype(F32), 0.0))
        )
        total = total + lax.dot_general(stack.astype(BF16), pick, NT, preferred_element_type=F32)
    surface_ref[...] = total[0:1] + total[1:2] + total[2:3]


def params(mib):
    return pltpu.CompilerParams(vmem_limit_bytes=mib * MIB)


def vmem(count):
    return [pl.BlockSpec(memory_space=pltpu.VMEM)] * count


def body(
    planck_source,
    absorber_path,
    cloud_depth,
    span_map,
    surface_source,
    interp_index,
    interp_weight,
    sunlit,
    sw_slot,
    cos_zenith,
    albedo,
    table_lw,
    table_sw,
    planck_frac,
    solar_weight,
):
    columns = span_map.shape[0]
    owners = lax.axis_size("col")
    devices = lax.axis_size("dyn") * owners
    slots = devices * CAP
    g_lw, g_sw = table_lw.shape[0], table_sw.shape[0]

    def row(x):
        return x.reshape(1, -1)

    send, slot = pl.pallas_call(
        pack_kernel,
        out_shape=(jax.ShapeDtypeStruct((slots, 128), I16), jax.ShapeDtypeStruct((1, columns), I32)),
        in_specs=vmem(4),
        out_specs=tuple(vmem(2)),
        compiler_params=params(60),
        name="pack",
    )(planck_source, absorber_path, cloud_depth, row(span_map))
    early_units = LEV // (2 * GROUP) * (columns // BLOCK)
    units = 4 // EARLY
    early = pl.pallas_call(
        absorb_kernel,
        grid=(early_units // units,),
        out_shape=jax.ShapeDtypeStruct((early_units, g_lw + g_sw, EARLY * BLOCK), F32),
        in_specs=vmem(4),
        out_specs=pl.BlockSpec((units, g_lw + g_sw, EARLY * BLOCK), lambda i: (i, 0, 0)),
        scratch_shapes=[
            pltpu.VMEM((4 * LEV, columns), F32),
            pltpu.VMEM((g_lw + g_sw, NTAB), BF16),
            pltpu.VMEM((NTAB, units * EARLY * BLOCK), BF16),
        ],
        compiler_params=params(60),
        cost_estimate=pl.CostEstimate(
            flops=2 * (g_lw + g_sw) * NTAB * early_units * EARLY * BLOCK,
            bytes_accessed=4 * (g_lw + g_sw) * early_units * EARLY * BLOCK,
            transcendentals=0,
        ),
        name="absorb",
    )(interp_index, interp_weight, table_lw, table_sw)
    recv = lax.all_to_all(send.reshape(devices, CAP, 128), ("dyn", "col"), 0, 0, tiled=True)
    back = pl.pallas_call(
        partial(radiation_kernel, owners),
        out_shape=jax.ShapeDtypeStruct((slots, 128), I16),
        in_specs=vmem(1) + [pl.BlockSpec(memory_space=pl.ANY)] + vmem(11),
        out_specs=vmem(1)[0],
        scratch_shapes=[
            pltpu.VMEM((3 * LEV, columns), F32),
            pltpu.VMEM((4 * LEV, columns), F32),
            pltpu.VMEM((40, columns), F32),
            pltpu.VMEM((LEV, columns), F32),
            pltpu.VMEM((g_lw + g_sw, KPAD), BF16),
            pltpu.VMEM((KPAD, GROUP * BLOCK), BF16),
            pltpu.VMEM((KPAD, (GROUP - EARLY) * BLOCK), BF16),
            pltpu.VMEM((g_lw + g_sw, GROUP * BLOCK), F32),
            pltpu.VMEM((g_lw + g_sw, (GROUP - EARLY) * BLOCK), F32),
            pltpu.VMEM((2, LEV, g_lw + g_sw, BLOCK), F32),
            pltpu.VMEM((g_lw, BLOCK), F32),
            pltpu.VMEM((g_sw, BLOCK), F32),
            pltpu.VMEM((g_lw, BLOCK), F32),
            pltpu.VMEM((g_sw, BLOCK), F32),
            pltpu.VMEM((8, BLOCK), F32),
            pltpu.VMEM((g_lw, BLOCK), F32),
            pltpu.VMEM((g_sw, BLOCK), F32),
            pltpu.VMEM((2 * LEV, columns), F32),
            pltpu.VMEM((8, columns), F32),
            pltpu.VMEM((2, g_lw + g_sw, EARLY * BLOCK), F32),
            pltpu.SemaphoreType.DMA((2,)),
        ],
        compiler_params=params(50),
        name="radiation",
    )(
        recv.reshape(slots, 128),
        early,
        row(surface_source),
        interp_index,
        interp_weight,
        row(sunlit),
        row(sw_slot),
        row(cos_zenith),
        row(albedo),
        table_lw,
        table_sw,
        row(planck_frac),
        row(solar_weight),
    )
    home = lax.all_to_all(back.reshape(devices, CAP, 128), ("dyn", "col"), 0, 0, tiled=True)
    heating_lw, heating_sw, surface = pl.pallas_call(
        home_kernel,
        out_shape=(jax.ShapeDtypeStruct((LEV, columns), F32),) * 2
        + (jax.ShapeDtypeStruct((1, columns // 2), F32),),
        in_specs=vmem(2),
        out_specs=tuple(vmem(3)),
        compiler_params=params(16),
        name="home",
    )(home.reshape(slots, 128), slot)
    return (heating_lw, heating_sw, surface.reshape(-1))


def solution(mesh):
    columns = P(None, ("dyn", "col"))
    flat = P(("dyn", "col"))
    in_specs = (
        columns, columns, columns, flat, flat, columns, P(None, None, ("dyn", "col")),
        flat, flat, flat, flat, P(), P(), P(), P(),
    )
    out_specs = (columns, columns, flat)
    return jax.shard_map(body, mesh=mesh, in_specs=in_specs, out_specs=out_specs, check_vma=False)
```
